256 devices in a mesh: group: 16 (over z_lo, y, core), tile: 16 (over x, z_hi).
Axes of the slice: x: 4, y: 4, z: 8 (z_hi: 4, z_lo: 2; z = z_hi * 2 + z_lo), core: 2. Of those that a mesh axis runs over, the one named last changes fastest.
Arguments:
- fields: float32 [16, 3, 8, 256, 256], P('group', None, None, 'tile'), may hold values from -6 to 6
- sample_index: int32 [16, 3], P('group'), may hold values from 0 to 3
- stencil: int32 [4, 256, 128], replicated, may hold values from 0 to 8191, as said below
- stencil_weight: float32 [4, 256, 128], replicated, may hold values from 0 to 1, as said below
Outputs:
- new_fields: float32 [16, 3, 8, 256, 256], P('group', None, None, 'tile')
The draws below stay inside these ranges and needn't reach their ends.
Inputs may be any that keep to these rules, and one draw needn't show every extreme that they name: `sample_index`: column 0 is a group's yaw index, column 1 its spacing index, column 2 its veer index. `stencil`: entry [a, y, x * 4 + k] is a flat index row * 32 + column into the outflow band for the k-th point of fringe cell (y, x) at yaw index a; the 4 points of one cell lie in two cyclically neighbouring rows and two neighbouring columns. `stencil_weight`: the 4 weights of each fringe cell are bilinear and sum to one.
All inputs are finite; a program needn't handle non-finite values.
Results may differ from the reference program's by a relative error of at most 0.0003.
Values sent between devices are 32-bit elements; how exact they have to be, the bound alone decides.
No kernel may reach another device: no remote copies, remote signals or barrier semaphores. Data moves between devices by JAX's collectives and lax.ppermute only.
A program may use at most 64 MiB of HBM per device.

```python
import jax
import jax.numpy as jnp
from jax import lax

COMP = 3
LEV = 8
CY = 16
NX = 256
FR = 32
STEN = 4
NYAW = 4
GROUPS = 16
NY = 256


def draw_stencil(key, part):
    keys = jax.random.split(key, 2 + NYAW)
    remap = jnp.stack([jax.random.permutation(keys[2 + yaw_slot], NY).astype(jnp.int32) for yaw_slot in range(NYAW)])
    remap = remap[:, :, None, None]
    yaw_ids = jnp.arange(NYAW, dtype=jnp.int32)[:, None, None, None]
    depth_ids = jnp.arange(FR, dtype=jnp.int32)[None, None, :, None]
    jitter_row = jax.random.randint(keys[0], (NYAW, NY, FR, 1), 0, 3, dtype=jnp.int32)
    jitter_col = jax.random.randint(keys[1], (NYAW, NY, FR, 1), -1, 2, dtype=jnp.int32)
    base_row = remap + (2 * yaw_ids - 3) * depth_ids // 4 + jitter_row
    base_col = jnp.clip(depth_ids + jitter_col, 0, FR - 2)
    row_offset = jnp.array([0, 1, 0, 1], dtype=jnp.int32)[None, None, None, :]
    col_offset = jnp.array([0, 0, 1, 1], dtype=jnp.int32)[None, None, None, :]
    flat_index = (base_row + row_offset) % NY * FR + base_col + col_offset
    return flat_index.reshape(NYAW, NY, FR * STEN).astype(jnp.int32)


def draw_stencil_weight(key, part):
    keys = jax.random.split(key, 2)
    frac_row = jax.random.uniform(keys[0], (NYAW, NY, FR, 1), jnp.float32)
    frac_col = jax.random.uniform(keys[1], (NYAW, NY, FR, 1), jnp.float32)
    row_part = jnp.concatenate([1.0 - frac_row, frac_row, 1.0 - frac_row, frac_row], axis=3)
    col_part = jnp.concatenate([1.0 - frac_col, 1.0 - frac_col, frac_col, frac_col], axis=3)
    return (row_part * col_part).reshape(NYAW, NY, FR * STEN).astype(jnp.float32)


def place_ends(values, own_key, smallest, high):
    dims = values.shape
    index_at = [jax.random.randint(jax.random.fold_in(own_key, axis), (), 0, dims[axis]) for axis in range(len(dims))]
    values = values.at[tuple(index_at)].set(smallest)
    longest = dims.index(max(dims))
    index_at[longest] = (index_at[longest] + 1) % dims[longest]
    return values.at[tuple(index_at)].set(high)


def steps_of(rng, shape, shards, low, largest):
    gain = 1.0
    for dim, blocks in shards:
        steps = jax.random.uniform(jax.random.fold_in(jax.random.fold_in(rng, 6), dim), (blocks,), jnp.float32, low / len(shards), largest / len(shards))
        gain = gain * jnp.repeat(jnp.exp(steps), shape[dim] // blocks).reshape((-1,) + (1,) * (len(shape) - 1 - dim))
    return gain


def centred(key, extent, scale, limit, pieces=(), kind=jnp.bfloat16):
    result = scale * jax.random.normal(key, extent, jnp.float32)
    if pieces:
        result = result * steps_of(key, extent, pieces, -0.22, 0.18)
    return jnp.clip(result, -limit, limit).astype(kind)


def setup_inputs(seed: int = 0) -> dict:
    splits = jax.random.split(jax.random.key(seed), 5)
    return {
        "fields": centred(splits[0], (GROUPS, COMP, LEV, NY, NX), 1.0, 6.0, ((0, 16), (3, 16)), jnp.float32),
        "sample_index": place_ends(jax.random.randint(splits[1], (GROUPS, 3), 0, NYAW), jax.random.fold_in(splits[1], 1), 0, NYAW - 1).astype(jnp.int32),
        "stencil": draw_stencil(jax.random.fold_in(splits[4], 71), 0),
        "stencil_weight": draw_stencil_weight(jax.random.fold_in(splits[4], 71), 0),
    }


TIME_STEP = 0.2
LATERAL_NU = 0.5
VERTICAL_NU = 0.5
SIGMA_PEAK = 2.5
DRAG_COEFF = 1.0
YAW_STEP = 0.2


def fringe_rate():
    column_ids = jnp.arange(FR, dtype=jnp.int32).astype(jnp.float32)
    return SIGMA_PEAK * 4.0 * (column_ids + 1.0) * (FR - column_ids) / float((FR + 1) ** 2)


def turbine_mask(spacing_index, row_start, row_count, width):
    column_ids = jnp.arange(width, dtype=jnp.int32)
    spacing = (spacing_index + 2) * (width // 32)
    first_col = FR + width // 16
    along_x = (column_ids >= first_col) & (column_ids < width - width // 16) & ((column_ids - first_col) % spacing == 0)
    row_ids = row_start + jnp.arange(row_count, dtype=jnp.int32)
    within = row_ids % CY
    along_y = (within >= CY * 3 // 8) & (within < CY * 5 // 8)
    level_ids = jnp.arange(LEV, dtype=jnp.int32)
    along_z = (level_ids >= 1) & (level_ids <= LEV // 2)
    joined = along_z[:, None, None] & along_y[None, :, None] & along_x[None, None, :]
    return joined.astype(jnp.float32)[None]


def rotate(planar, yaw_index):
    angle = YAW_STEP * (yaw_index.astype(jnp.float32) - 1.5)
    cosine = jnp.cos(angle)
    sine = jnp.sin(angle)
    return jnp.stack([cosine * planar[0] - sine * planar[1], sine * planar[0] + cosine * planar[1], planar[2]])


def shifted_sources(table_rows, veer_index, total_rows):
    source = table_rows.reshape(-1)
    source_row = source // FR
    source_col = source % FR
    level_ids = jnp.arange(LEV, dtype=jnp.int32)
    veer_shift = veer_index * (level_ids + 1) * (CY // 4)
    return ((source_row[None, :] + veer_shift[:, None]) % total_rows) * FR + source_col[None, :]


def tendency(current, side_values, relax_target, relax_rate, turbines, farm_flag):
    east_side, west_side, north_side, south_side = side_values
    stream = current[0:1]
    cross = current[1:2]
    advect = 0.5 * (stream * (east_side - west_side) + cross * (north_side - south_side))
    lateral = LATERAL_NU * (east_side + west_side + north_side + south_side - 4.0 * current)
    below = jnp.concatenate([-current[:, :1], current[:, :-1]], axis=1)
    above = jnp.concatenate([current[:, 1:], current[:, -1:]], axis=1)
    vertical = VERTICAL_NU * (above - 2.0 * current + below)
    drag = -DRAG_COEFF * turbines * jnp.abs(stream) * current
    relax = relax_rate * (relax_target - current[..., :FR])
    relax_full = jnp.concatenate([relax, jnp.zeros(current[..., FR:].shape, jnp.float32)], axis=3)
    return lateral + vertical - advect + farm_flag * (drag + relax_full)


def advance(initial, relax_target, turbines, farm_flag, neighbours):
    relax_rate = fringe_rate()
    predicted = initial + TIME_STEP * tendency(initial, neighbours(initial), relax_target, relax_rate, turbines, farm_flag)
    corrected = tendency(predicted, neighbours(predicted), relax_target, relax_rate, turbines, farm_flag)
    return 0.5 * (initial + predicted + TIME_STEP * corrected)


def roll_sides(current):
    return (jnp.roll(current, -1, axis=3), jnp.roll(current, 1, axis=3), jnp.roll(current, -1, axis=2), jnp.roll(current, 1, axis=2))


def reference(fields, sample_index, stencil, stencil_weight):
    outflow_band = fields[0, :, :, :, NX - FR:].reshape(COMP, LEV, NY * FR)
    group_ids = jnp.arange(GROUPS, dtype=jnp.int32)

    def one_group(inputs):
        current, indices, group_id = inputs
        yaw_index = indices[0]
        yaw_table = lax.dynamic_index_in_dim(stencil, yaw_index, 0, keepdims=False)
        weight_table = lax.dynamic_index_in_dim(stencil_weight, yaw_index, 0, keepdims=False)
        moved = shifted_sources(yaw_table, indices[2], NY)
        picked = jnp.take_along_axis(outflow_band, jnp.broadcast_to(moved[None], (COMP, LEV, moved.shape[1])), axis=2)
        planar = jnp.sum((picked * weight_table.reshape(-1)).reshape(COMP, LEV, NY, FR, STEN), axis=4)
        relax_target = rotate(planar, yaw_index)
        turbines = turbine_mask(indices[1], 0, NY, NX)
        farm_flag = (group_id > 0).astype(jnp.float32)
        return advance(current, relax_target, turbines, farm_flag, roll_sides)

    return lax.map(one_group, (fields, sample_index, group_ids))
```

```python
import jax
import jax.numpy as jnp
import numpy as np
from jax import lax
from jax.experimental import pallas as pl
from jax.experimental.pallas import tpu as pltpu
from jax.sharding import PartitionSpec as P

COMP = 3
LEV = 8
CY = 16
NX = 256
FR = 32
STEN = 4
NYAW = 4
GROUPS = 16
NY = 256
TILES = NY // CY
HALF = CY // 2
LANES = 128
VC = NYAW * COMP

TIME_STEP = 0.2
YAW_STEP = 0.2
SIGMA_PEAK = 2.5

F32 = jnp.float32
BF16 = jnp.bfloat16
VMEM = pl.BlockSpec(memory_space=pltpu.VMEM)
SMEM = pl.BlockSpec(memory_space=pltpu.SMEM)
ANY = pl.BlockSpec(memory_space=pl.ANY)


def params():
    return pltpu.CompilerParams(vmem_limit_bytes=48 * 1024 * 1024)


def cost(flops, moved):
    return pl.CostEstimate(flops=flops, bytes_accessed=moved, transcendentals=0)


def shape(*dims, dtype=F32):
    return jax.ShapeDtypeStruct(dims, dtype)


def lane_iota(rows, lanes):
    return lax.broadcasted_iota(jnp.int32, (rows, lanes), 1)


def row_iota(rows, lanes):
    return lax.broadcasted_iota(jnp.int32, (rows, lanes), 0)


def pack_kernel(sample_ref, fields_ref, msg_ref, low_ref, high_ref):
    combo = (sample_ref[0, 2] * NYAW + sample_ref[0, 0]).astype(F32)
    lane = lane_iota(CY, LANES)
    for lev in range(LEV):
        packed = jnp.full((CY, LANES), combo, F32)
        for comp in range(COMP):
            band = pltpu.roll(fields_ref[0, comp, lev, :, NX - LANES :], (comp + 1) * FR, 1)
            packed = jnp.where((lane >= comp * FR) & (lane < (comp + 1) * FR), band, packed)
        msg_ref[2 * lev] = packed
        msg_ref[2 * lev + 1] = packed
        for comp in range(COMP):
            for row in range(2):
                low_ref[comp, row, lev : lev + 1, :] = fields_ref[0, comp, lev, row : row + 1, :]
                high_ref[comp, row, lev : lev + 1, :] = fields_ref[
                    0, comp, lev, CY - 2 + row : CY - 1 + row, :
                ]


def prepare_kernel(
    stencil_ref, weight_ref, base_ref, key_ref, out_weight_ref, sten, wts, sten_x, wts_x, perm, sems
):
    half = lax.axis_index("group") % 2
    start = lax.axis_index("tile") * CY + half * HALF
    beyond = (start + jnp.where(half == 0, NY - HALF, HALF)) % NY
    start = pl.multiple_of(start, HALF)
    beyond = pl.multiple_of(beyond, HALF)
    copies = [
        pltpu.make_async_copy(stencil_ref.at[:, pl.ds(start, HALF), :], sten, sems.at[0]),
        pltpu.make_async_copy(weight_ref.at[:, pl.ds(start, HALF), :], wts, sems.at[1]),
        pltpu.make_async_copy(stencil_ref.at[:, pl.ds(beyond, HALF), :], sten_x, sems.at[2]),
        pltpu.make_async_copy(weight_ref.at[:, pl.ds(beyond, HALF), :], wts_x, sems.at[3]),
    ]
    for copy in copies:
        copy.start()
    source = row_iota(512, 512)
    target = (source % 4) * LANES + (source // LANES) * FR + (source % LANES) // 4
    perm[...] = jnp.where(target == lane_iota(512, 512), 1.0, 0.0).astype(BF16)
    for copy in copies:
        copy.wait()

    def gathered(main, extra):
        parts = []
        for part in range(4):
            rows = [main[yaw, part + 4 * j : part + 4 * j + 1, :] for yaw in range(NYAW) for j in range(2)]
            outer = jnp.where(half == 0, extra[part, HALF - 1 : HALF, :], extra[part, 0:1, :])
            rows.append(outer)
            rows.append(jnp.zeros((7, LANES), outer.dtype))
            parts.append(jnp.concatenate(rows, axis=0))
        return jnp.concatenate(parts, axis=1)

    index = gathered(sten, sten_x)
    weight = gathered(wts, wts_x)
    first = weight.astype(BF16)
    rest = weight - first.astype(F32)
    second = rest.astype(BF16)
    third = (rest - second.astype(F32)).astype(BF16)
    source_row = (index >> 5).astype(F32).astype(BF16)
    source_col = (index & 31).astype(F32).astype(BF16)
    stacked = jnp.concatenate([source_row, source_col, first, second, third], axis=0)
    sorted_ = jnp.dot(stacked, perm[...], preferred_element_type=F32)
    weight = (sorted_[32:48] + sorted_[48:64]) + sorted_[64:80]
    rows = [sorted_[0:16, k * LANES : (k + 1) * LANES] for k in range(STEN)]
    cols = [sorted_[16:32, k * LANES : (k + 1) * LANES] for k in range(STEN)]
    below = jnp.zeros((16, LANES), F32)
    for k in range(1, STEN):
        delta = rows[k] - rows[0]
        below = jnp.where((delta == -1.0) | (delta == NY - 1.0), 1.0, below)
    base = rows[0] - below
    base = jnp.where(base < 0.0, base + NY, base)
    base_ref[...] = base.astype(jnp.int32)
    for k in range(STEN):
        offset = rows[k] - base
        offset = jnp.where(offset < 0.0, offset + NY, offset)
        key_ref[k] = (offset * FR + cols[k]).astype(jnp.int32)
        out_weight_ref[k] = weight[:, k * LANES : (k + 1) * LANES]


def interpolate_kernel(
    band_ref, asked_ref, base_ref, key_ref, weight_ref, out_ref, table, hot, product, picked, outer
):
    level = lax.axis_index("group") // 2
    band = band_ref[...].reshape(NY, LANES).T[: COMP * FR]
    for veer in range(NYAW):
        for step in range(2):
            shift = (NY - (veer * (level + 1) * (CY // 4) + step)) % NY
            moved = band if veer + step == 0 else pltpu.roll(band, shift, 1)
            upper = moved.astype(BF16)
            lower = (moved - upper.astype(F32)).astype(BF16)
            for comp in range(COMP):
                at = ((veer * COMP + comp) * 2 + step) * FR
                table[at : at + FR, 0:NY] = upper[comp * FR : (comp + 1) * FR]
                table[at : at + FR, NY : 2 * NY] = lower[comp * FR : (comp + 1) * FR]
    row_ids = row_iota(NY, LANES)
    key_ids = row_iota(2 * FR, LANES)
    for pair in range(5):
        cells = [cell for cell in (2 * pair, 2 * pair + 1) if cell <= 2 * NYAW]
        width = LANES * len(cells)
        for at, cell in enumerate(cells):
            ones = jnp.where(row_ids == base_ref[cell : cell + 1, :], 1.0, 0.0).astype(BF16)
            hot[0:NY, at * LANES : (at + 1) * LANES] = ones
            hot[NY : 2 * NY, at * LANES : (at + 1) * LANES] = ones
        product[:, 0:width] = jnp.dot(table[...], hot[:, 0:width], preferred_element_type=F32)
        for at, cell in enumerate(cells):
            weights = jnp.zeros((2 * FR, LANES), F32)
            for k in range(STEN):
                weights = weights + jnp.where(
                    key_ids == key_ref[k, cell : cell + 1, :], weight_ref[k, cell : cell + 1, :], 0.0
                )
            for one in range(VC):
                value = jnp.sum(
                    product[one * 2 * FR : (one + 1) * 2 * FR, at * LANES : (at + 1) * LANES] * weights,
                    axis=0,
                    keepdims=True,
                )
                veer, comp = divmod(one, COMP)
                if cell < 2 * NYAW:
                    yaw, j = divmod(cell, 2)
                    picked[veer * NYAW + yaw, 2 * comp + j : 2 * comp + j + 1, :] = value
                else:
                    outer[one : one + 1, :] = value
    lane = lane_iota(1, LANES)
    rolled = [outer[...] if turn == 0 else pltpu.roll(outer[...], turn * FR, 1) for turn in range(4)]
    for veer in range(NYAW):
        for yaw in range(NYAW):
            rows = [
                rolled[(comp - yaw) % 4][veer * COMP + comp : veer * COMP + comp + 1] for comp in range(COMP)
            ]
            row = jnp.where(lane < FR, rows[0], jnp.where(lane < 2 * FR, rows[1], rows[2]))
            picked[veer * NYAW + yaw, 6:7, :] = row
            picked[veer * NYAW + yaw, 7:8, :] = row
    tile_lane = lane_iota(8, LANES)
    for group in range(GROUPS):
        asked = jnp.where(tile_lane >= COMP * FR, asked_ref[group, 0:8, :], 0.0)
        asked = asked + pltpu.roll(asked, FR, 1)
        asked = asked + pltpu.roll(asked, 2 * FR, 1)
        chosen = picked[0]
        for combo in range(1, NYAW * NYAW):
            chosen = jnp.where(asked == float(combo), picked[combo], chosen)
        out_ref[group] = chosen


def step_kernel(
    sample_ref, fields_ref, planar_ref, low_ref, high_ref, before_ref, after_ref, out_ref, target, pred, edge
):
    flag = jnp.where(lax.axis_index("group") > 0, TIME_STEP, 0.0).astype(F32)
    yaw = sample_ref[0, 0]
    angles = np.float32(YAW_STEP) * (np.arange(NYAW, dtype=np.float32) - np.float32(1.5))
    cosine = jnp.float32(np.cos(angles[0]))
    sine = jnp.float32(np.sin(angles[0]))
    for at in range(1, NYAW):
        cosine = jnp.where(yaw == at, jnp.float32(np.cos(angles[at])), cosine)
        sine = jnp.where(yaw == at, jnp.float32(np.sin(angles[at])), sine)
    spacing = ((sample_ref[0, 1] + 2) * (NX // 32)).astype(F32)

    column = lane_iota(1, LANES).astype(F32)
    rate = SIGMA_PEAK * 4.0 * (column + 1.0) * (FR - column) / float((FR + 1) ** 2)
    rate = jnp.where(column < FR, rate, 0.0) * flag
    rate = jnp.concatenate([rate, jnp.zeros((1, LANES), F32)], axis=1)

    column = lane_iota(CY, NX).astype(F32)
    row = row_iota(CY, NX)
    first_col = float(FR + NX // 16)
    away = column - first_col
    count = jnp.floor(away / spacing + 0.5)
    mask = (column >= first_col) & (column < NX - NX // 16) & (count * spacing == away)
    mask = mask & (row >= CY * 3 // 8) & (row < CY * 5 // 8)
    drag = jnp.where(mask, flag, 0.0)

    for lev in range(LEV):
        for half in range(2):
            packed = planar_ref[2 * lev + half]
            for part in range(4):
                turned = packed if part == 0 else pltpu.roll(packed, LANES - part * FR, 1)
                for comp in range(COMP):
                    for j in range(2):
                        at = half * HALF + 4 * j + part
                        target[comp, lev, at : at + 1, :] = turned[2 * comp + j : 2 * comp + j + 1]
        first, second = target[0, lev], target[1, lev]
        target[0, lev] = cosine * first - sine * second
        target[1, lev] = sine * first + cosine * second

    def west_east(u):
        return pltpu.roll(u, 1, 1), pltpu.roll(u, NX - 1, 1)

    def padded(aim):
        return jnp.concatenate([aim, jnp.zeros(aim.shape, F32)], axis=1)

    def change(u, stream, cross, north, south, above, below, aim, drag_rate):
        west, east = west_east(u)
        total = (east + west) + (north + south) + (above + below) - 6.0 * u
        total = total - stream * (east - west) - cross * (north - south)
        total = 0.1 * total + rate * (padded(aim) - u)
        if drag_rate is not None:
            total = total - drag_rate * u
        return total

    level_ids = row_iota(LEV, NX)
    for side in range(2):
        if side == 0:
            here = [before_ref[comp, 1] for comp in range(COMP)]
            south = [before_ref[comp, 0] for comp in range(COMP)]
            north = [low_ref[comp, 0] for comp in range(COMP)]
        else:
            here = [after_ref[comp, 0] for comp in range(COMP)]
            south = [high_ref[comp, 1] for comp in range(COMP)]
            north = [after_ref[comp, 1] for comp in range(COMP)]
        packed = jnp.concatenate([planar_ref[2 * lev + side, 6:7, :] for lev in range(LEV)], axis=0)
        aims = [packed] + [pltpu.roll(packed, LANES - comp * FR, 1) for comp in range(1, COMP)]
        aims = [cosine * aims[0] - sine * aims[1], sine * aims[0] + cosine * aims[1], aims[2]]
        for comp in range(COMP):
            u = here[comp]
            below = jnp.where(level_ids == 0, -u, pltpu.roll(u, 1, 0))
            above = jnp.where(level_ids == LEV - 1, u, pltpu.roll(u, LEV - 1, 0))
            edge[side, comp] = u + change(
                u, here[0], here[1], north[comp], south[comp], above, below, aims[comp], None
            )

    def stage(read, low_row, high_row, write):
        for lev in range(LEV):
            stream, cross = read(0, lev), read(1, lev)
            drag_rate = drag * jnp.abs(stream) if 1 <= lev <= LEV // 2 else None
            for comp in range(COMP):
                u = (stream, cross)[comp] if comp < 2 else read(comp, lev)
                below = -u if lev == 0 else read(comp, lev - 1)
                above = u if lev == LEV - 1 else read(comp, lev + 1)
                north = jnp.where(row == CY - 1, high_row(comp, lev), pltpu.roll(u, CY - 1, 0))
                south = jnp.where(row == 0, low_row(comp, lev), pltpu.roll(u, 1, 0))
                moved = change(u, stream, cross, north, south, above, below, target[comp, lev], drag_rate)
                write(comp, lev, u, moved)

    def write_pred(comp, lev, u, moved):
        pred[comp, lev] = u + moved

    def write_out(comp, lev, u, moved):
        out_ref[0, comp, lev] = 0.5 * (fields_ref[0, comp, lev] + u + moved)

    stage(
        lambda comp, lev: fields_ref[0, comp, lev],
        lambda comp, lev: before_ref[comp, 1, lev : lev + 1, :],
        lambda comp, lev: after_ref[comp, 0, lev : lev + 1, :],
        write_pred,
    )
    stage(
        lambda comp, lev: pred[comp, lev],
        lambda comp, lev: edge[0, comp, lev : lev + 1, :],
        lambda comp, lev: edge[1, comp, lev : lev + 1, :],
        write_out,
    )


def local(fields, sample_index, stencil, stencil_weight):
    message, low, high = pl.pallas_call(
        pack_kernel,
        out_shape=(shape(GROUPS, CY, LANES), shape(COMP, 2, LEV, NX), shape(COMP, 2, LEV, NX)),
        in_specs=[SMEM, VMEM],
        out_specs=(VMEM, VMEM, VMEM),
        compiler_params=params(),
        name="pack",
    )(sample_index, fields)
    up = [(i, (i + 1) % TILES) for i in range(TILES)]
    down = [(j, i) for i, j in up]
    before = lax.ppermute(high, "tile", up)
    after = lax.ppermute(low, "tile", down)
    asked = lax.all_to_all(message, "group", 0, 0, tiled=True)
    base, key, weight = pl.pallas_call(
        prepare_kernel,
        out_shape=(
            shape(16, LANES, dtype=jnp.int32),
            shape(STEN, 16, LANES, dtype=jnp.int32),
            shape(STEN, 16, LANES),
        ),
        in_specs=[ANY, ANY],
        out_specs=(VMEM, VMEM, VMEM),
        scratch_shapes=[
            pltpu.VMEM((NYAW, HALF, LANES), jnp.int32),
            pltpu.VMEM((NYAW, HALF, LANES), F32),
            pltpu.VMEM((NYAW, HALF, LANES), jnp.int32),
            pltpu.VMEM((NYAW, HALF, LANES), F32),
            pltpu.VMEM((512, 512), BF16),
            pltpu.SemaphoreType.DMA((4,)),
        ],
        compiler_params=params(),
        cost_estimate=cost(2 * 80 * 512 * 512, 200_000),
        name="prepare",
    )(stencil, stencil_weight)
    band = lax.all_to_all(
        jnp.broadcast_to(asked[0:1], (TILES, CY, LANES)), "tile", 0, 0, tiled=True
    )
    answers = pl.pallas_call(
        interpolate_kernel,
        out_shape=shape(GROUPS, 8, LANES),
        in_specs=[VMEM] * 5,
        out_specs=VMEM,
        scratch_shapes=[
            pltpu.VMEM((VC * 2 * FR, 2 * NY), BF16),
            pltpu.VMEM((2 * NY, 2 * LANES), BF16),
            pltpu.VMEM((VC * 2 * FR, 2 * LANES), F32),
            pltpu.VMEM((NYAW * NYAW, 8, LANES), F32),
            pltpu.VMEM((16, LANES), F32),
        ],
        compiler_params=params(),
        name="interpolate",
    )(band, asked, base, key, weight)
    planar = lax.all_to_all(answers, "group", 0, 0, tiled=True)
    return pl.pallas_call(
        step_kernel,
        out_shape=shape(1, COMP, LEV, CY, NX),
        in_specs=[SMEM] + [VMEM] * 6,
        out_specs=VMEM,
        scratch_shapes=[
            pltpu.VMEM((COMP, LEV, CY, LANES), F32),
            pltpu.VMEM((COMP, LEV, CY, NX), F32),
            pltpu.VMEM((2, COMP, LEV, NX), F32),
        ],
        compiler_params=params(),
        name="step",
    )(sample_index, fields, planar, low, high, before, after)


def solution(mesh):
    in_specs = (P("group", None, None, "tile", None), P("group", None), P(), P())
    out_specs = P("group", None, None, "tile", None)
    return jax.shard_map(local, mesh=mesh, in_specs=in_specs, out_specs=out_specs, check_vma=False)
```

```python
import jax
import jax.numpy as jnp
import numpy as np
from jax import lax
from jax.experimental import pallas as pl
from jax.experimental.pallas import tpu as pltpu
from jax.sharding import PartitionSpec as P

COMP = 3
LEV = 8
CY = 16
NX = 256
FR = 32
PACK_KIB = 60000
STEN = 4
NYAW = 4
GROUPS = 16
NY = 256
TILES = NY // CY
HALF = CY // 2
LANES = 128
VC = NYAW * COMP

TIME_STEP = 0.2
YAW_STEP = 0.2
SIGMA_PEAK = 2.5

F32 = jnp.float32
BF16 = jnp.bfloat16
VMEM = pl.BlockSpec(memory_space=pltpu.VMEM)
SMEM = pl.BlockSpec(memory_space=pltpu.SMEM)
HBM = pl.BlockSpec(memory_space=pltpu.HBM)


def params(kib=48 * 1024):
    return pltpu.CompilerParams(vmem_limit_bytes=kib * 1024)


def cost(flops, moved):
    return pl.CostEstimate(flops=flops, bytes_accessed=moved, transcendentals=0)


def shape(*dims, dtype=F32):
    return jax.ShapeDtypeStruct(dims, dtype)


def lane_iota(rows, lanes):
    return lax.broadcasted_iota(jnp.int32, (rows, lanes), 1)


def row_iota(rows, lanes):
    return lax.broadcasted_iota(jnp.int32, (rows, lanes), 0)


def pack_kernel(sample_hbm, fields_hbm, msg_ref, low_ref, high_ref, sample_ref, fields_ref, sems):
    sample_copy = pltpu.make_async_copy(sample_hbm, sample_ref, sems.at[0])
    sample_copy.start()
    halves = [pl.ds(NX - LANES, LANES), pl.ds(0, LANES)]
    copies = [
        [
            pltpu.make_async_copy(
                fields_hbm.at[0, comp, :, :, lanes], fields_ref.at[comp, :, :, lanes], sems.at[1 + 3 * at + comp]
            )
            for comp in range(COMP)
        ]
        for at, lanes in enumerate(halves)
    ]
    for part in copies:
        for copy in part:
            copy.start()
    for copy in copies[0]:
        copy.wait()
    sample_copy.wait()
    combo = (sample_ref[0, 2] * NYAW + sample_ref[0, 0]).astype(F32)
    lane = lane_iota(CY, LANES)
    for lev in range(LEV):
        packed = jnp.full((CY, LANES), combo, F32)
        for comp in range(COMP):
            band = pltpu.roll(fields_ref[comp, lev, :, NX - LANES :], (comp + 1) * FR, 1)
            packed = jnp.where((lane >= comp * FR) & (lane < (comp + 1) * FR), band, packed)
        msg_ref[2 * lev] = packed
        msg_ref[2 * lev + 1] = packed
    for copy in copies[1]:
        copy.wait()
    for lev in range(LEV):
        for comp in range(COMP):
            for row in range(2):
                low_ref[comp, row, lev : lev + 1, :] = fields_ref[comp, lev, row : row + 1, :]
                high_ref[comp, row, lev : lev + 1, :] = fields_ref[
                    comp, lev, CY - 2 + row : CY - 1 + row, :
                ]


def prepare_kernel(
    stencil_ref, weight_ref, base_ref, key_ref, out_weight_ref, sten, wts, sten_x, wts_x, perm, sems
):
    half = lax.axis_index("group") % 2
    start = lax.axis_index("tile") * CY + half * HALF
    beyond = (start + jnp.where(half == 0, NY - HALF, HALF)) % NY
    start = pl.multiple_of(start, HALF)
    beyond = pl.multiple_of(beyond, HALF)
    copies = [
        pltpu.make_async_copy(stencil_ref.at[:, pl.ds(start, HALF), :], sten, sems.at[0]),
        pltpu.make_async_copy(weight_ref.at[:, pl.ds(start, HALF), :], wts, sems.at[1]),
        pltpu.make_async_copy(stencil_ref.at[:, pl.ds(beyond, HALF), :], sten_x, sems.at[2]),
        pltpu.make_async_copy(weight_ref.at[:, pl.ds(beyond, HALF), :], wts_x, sems.at[3]),
    ]
    for copy in copies:
        copy.start()
    source = row_iota(512, 512)
    target = (source % 4) * LANES + (source // LANES) * FR + (source % LANES) // 4
    perm[...] = jnp.where(target == lane_iota(512, 512), 1.0, 0.0).astype(BF16)
    for copy in copies:
        copy.wait()

    def gathered(main, extra):
        parts = []
        for part in range(4):
            rows = [main[yaw, part + 4 * j : part + 4 * j + 1, :] for yaw in range(NYAW) for j in range(2)]
            outer = jnp.where(half == 0, extra[part, HALF - 1 : HALF, :], extra[part, 0:1, :])
            rows.append(outer)
            rows.append(jnp.zeros((7, LANES), outer.dtype))
            parts.append(jnp.concatenate(rows, axis=0))
        return jnp.concatenate(parts, axis=1)

    index = gathered(sten, sten_x)
    weight = gathered(wts, wts_x)
    first = weight.astype(BF16)
    rest = weight - first.astype(F32)
    second = rest.astype(BF16)
    third = (rest - second.astype(F32)).astype(BF16)
    source_row = (index >> 5).astype(F32).astype(BF16)
    source_col = (index & 31).astype(F32).astype(BF16)
    stacked = jnp.concatenate([source_row, source_col, first, second, third], axis=0)
    sorted_ = jnp.dot(stacked, perm[...], preferred_element_type=F32)
    weight = (sorted_[32:48] + sorted_[48:64]) + sorted_[64:80]
    rows = [sorted_[0:16, k * LANES : (k + 1) * LANES] for k in range(STEN)]
    cols = [sorted_[16:32, k * LANES : (k + 1) * LANES] for k in range(STEN)]
    below = jnp.zeros((16, LANES), F32)
    for k in range(1, STEN):
        delta = rows[k] - rows[0]
        below = jnp.where((delta == -1.0) | (delta == NY - 1.0), 1.0, below)
    base = rows[0] - below
    base = jnp.where(base < 0.0, base + NY, base)
    base_ref[...] = base.astype(jnp.int32)
    for k in range(STEN):
        offset = rows[k] - base
        offset = jnp.where(offset < 0.0, offset + NY, offset)
        key_ref[k] = (offset * FR + cols[k]).astype(jnp.int32)
        out_weight_ref[k] = weight[:, k * LANES : (k + 1) * LANES]


def interpolate_kernel(
    band_ref, asked_ref, base_ref, key_ref, weight_ref, out_ref, table, picked, outer
):
    level = lax.axis_index("group") // 2
    band = band_ref[...].reshape(NY, LANES).T[: COMP * FR]
    for veer in range(NYAW):
        for step in range(2):
            shift = (NY - (veer * (level + 1) * (CY // 4) + step)) % NY
            moved = band if veer + step == 0 else pltpu.roll(band, shift, 1)
            upper = moved.astype(BF16)
            lower = (moved - upper.astype(F32)).astype(BF16)
            for comp in range(COMP):
                at = ((veer * COMP + comp) * 2 + step) * FR
                table[at : at + FR, 0:NY] = upper[comp * FR : (comp + 1) * FR]
                table[at : at + FR, NY : 2 * NY] = lower[comp * FR : (comp + 1) * FR]
    row_ids = row_iota(NY, LANES)
    key_ids = row_iota(2 * FR, LANES)
    for pair in range(5):
        cells = [cell for cell in (2 * pair, 2 * pair + 1) if cell <= 2 * NYAW]
        ones = jnp.concatenate(
            [jnp.where(row_ids == base_ref[cell : cell + 1, :], 1.0, 0.0).astype(BF16) for cell in cells], axis=1
        )
        product = jnp.dot(table[...], jnp.concatenate([ones, ones], axis=0), preferred_element_type=F32)
        for at, cell in enumerate(cells):
            weights = jnp.zeros((2 * FR, LANES), F32)
            for k in range(STEN):
                weights = weights + jnp.where(
                    key_ids == key_ref[k, cell : cell + 1, :], weight_ref[k, cell : cell + 1, :], 0.0
                )
            for one in range(VC):
                value = jnp.sum(
                    product[one * 2 * FR : (one + 1) * 2 * FR, at * LANES : (at + 1) * LANES] * weights,
                    axis=0,
                    keepdims=True,
                )
                veer, comp = divmod(one, COMP)
                if cell < 2 * NYAW:
                    yaw, j = divmod(cell, 2)
                    picked[veer * NYAW + yaw, 2 * comp + j : 2 * comp + j + 1, :] = value
                else:
                    outer[one : one + 1, :] = value
    lane = lane_iota(1, LANES)
    rolled = [outer[...] if turn == 0 else pltpu.roll(outer[...], turn * FR, 1) for turn in range(4)]
    for veer in range(NYAW):
        for yaw in range(NYAW):
            rows = [
                rolled[(comp - yaw) % 4][veer * COMP + comp : veer * COMP + comp + 1] for comp in range(COMP)
            ]
            row = jnp.where(lane < FR, rows[0], jnp.where(lane < 2 * FR, rows[1], rows[2]))
            picked[veer * NYAW + yaw, 6:7, :] = row
            picked[veer * NYAW + yaw, 7:8, :] = row
    tile_lane = lane_iota(8, LANES)
    for group in range(GROUPS):
        asked = jnp.where(tile_lane >= COMP * FR, asked_ref[group, 0:8, :], 0.0)
        asked = asked + pltpu.roll(asked, FR, 1)
        asked = asked + pltpu.roll(asked, 2 * FR, 1)
        chosen = picked[0]
        for combo in range(1, NYAW * NYAW):
            chosen = jnp.where(asked == float(combo), picked[combo], chosen)
        out_ref[group] = chosen


def rates(flag, spacing):
    column = lane_iota(1, LANES).astype(F32)
    rate = SIGMA_PEAK * 4.0 * (column + 1.0) * (FR - column) / float((FR + 1) ** 2)
    rate = jnp.where(column < FR, rate, 0.0) * flag
    column = lane_iota(CY, NX).astype(F32)
    row = row_iota(CY, NX)
    first_col = float(FR + NX // 16)
    away = column - first_col
    count = jnp.floor(away / spacing + 0.5)
    mask = (column >= first_col) & (column < NX - NX // 16) & (count * spacing == away)
    mask = mask & (row >= CY * 3 // 8) & (row < CY * 5 // 8)
    return rate, jnp.where(mask, flag, 0.0)


def change(u, stream, cross, west, east, north, south, above, below):
    total = (east + west) + (north + south) + (above + below) - 6.0 * u
    return 0.1 * (total - stream * (east - west) - cross * (north - south))


def begin_kernel(
    sample_ref, fields_ref, low_ref, high_ref, before_ref, after_ref, pred_ref, edge_ref, right_ref
):
    flag = jnp.where(lax.axis_index("group") > 0, TIME_STEP, 0.0).astype(F32)
    spacing = ((sample_ref[0, 1] + 2) * (NX // 32)).astype(F32)
    rate, drag = rates(flag, spacing)
    rate = jnp.concatenate([rate, jnp.zeros((1, LANES), F32)], axis=1)
    row = row_iota(CY, NX)

    level_ids = row_iota(LEV, NX)
    for side in range(2):
        if side == 0:
            here = [before_ref[comp, 1] for comp in range(COMP)]
            south = [before_ref[comp, 0] for comp in range(COMP)]
            north = [low_ref[comp, 0] for comp in range(COMP)]
        else:
            here = [after_ref[comp, 0] for comp in range(COMP)]
            south = [high_ref[comp, 1] for comp in range(COMP)]
            north = [after_ref[comp, 1] for comp in range(COMP)]
        for comp in range(COMP):
            u = here[comp]
            below = jnp.where(level_ids == 0, -u, pltpu.roll(u, 1, 0))
            above = jnp.where(level_ids == LEV - 1, u, pltpu.roll(u, LEV - 1, 0))
            west, east = pltpu.roll(u, 1, 1), pltpu.roll(u, NX - 1, 1)
            moved = change(u, here[0], here[1], west, east, north[comp], south[comp], above, below)
            edge_ref[side, comp] = u + moved - rate * u

    for lev in range(LEV):
        stream, cross = fields_ref[0, 0, lev], fields_ref[0, 1, lev]
        loss = rate + drag * jnp.abs(stream) if 1 <= lev <= LEV // 2 else rate
        for comp in range(COMP):
            u = fields_ref[0, comp, lev]
            below = -u if lev == 0 else fields_ref[0, comp, lev - 1]
            above = u if lev == LEV - 1 else fields_ref[0, comp, lev + 1]
            north = jnp.where(row == CY - 1, after_ref[comp, 0, lev : lev + 1, :], pltpu.roll(u, CY - 1, 0))
            south = jnp.where(row == 0, before_ref[comp, 1, lev : lev + 1, :], pltpu.roll(u, 1, 0))
            west, east = pltpu.roll(u, 1, 1), pltpu.roll(u, NX - 1, 1)
            moved = change(u, stream, cross, west, east, north, south, above, below)
            pred_ref[comp, lev] = u + moved - loss * u

    row = row_iota(CY, LANES)
    lane = lane_iota(CY, LANES)
    for lev in range(LEV):
        stream, cross = pred_ref[0, lev, :, LANES:], pred_ref[1, lev, :, LANES:]
        for comp in range(COMP):
            u = pred_ref[comp, lev, :, LANES:]
            left = pred_ref[comp, lev, :, :LANES]
            below = -u if lev == 0 else pred_ref[comp, lev - 1, :, LANES:]
            above = u if lev == LEV - 1 else pred_ref[comp, lev + 1, :, LANES:]
            north = jnp.where(row == CY - 1, edge_ref[1, comp, lev : lev + 1, LANES:], pltpu.roll(u, CY - 1, 0))
            south = jnp.where(row == 0, edge_ref[0, comp, lev : lev + 1, LANES:], pltpu.roll(u, 1, 0))
            east = pltpu.roll(jnp.where(lane == 0, left, u), LANES - 1, 1)
            west = pltpu.roll(jnp.where(lane == LANES - 1, left, u), 1, 1)
            moved = change(u, stream, cross, west, east, north, south, above, below)
            if 1 <= lev <= LEV // 2:
                moved = moved - drag[:, LANES:] * jnp.abs(stream) * u
            right_ref[comp, lev] = 0.5 * (fields_ref[0, comp, lev, :, LANES:] + u + moved)


def finish_kernel(
    sample_ref, fields_ref, planar_ref, pred_ref, edge_ref, right_ref, out_ref, target, full, edge, result, sems
):
    flag = jnp.where(lax.axis_index("group") > 0, TIME_STEP, 0.0).astype(F32)
    yaw = sample_ref[0, 0]
    angles = np.float32(YAW_STEP) * (np.arange(NYAW, dtype=np.float32) - np.float32(1.5))
    cosine = jnp.float32(np.cos(angles[0]))
    sine = jnp.float32(np.sin(angles[0]))
    for at in range(1, NYAW):
        cosine = jnp.where(yaw == at, jnp.float32(np.cos(angles[at])), cosine)
        sine = jnp.where(yaw == at, jnp.float32(np.sin(angles[at])), sine)
    spacing = ((sample_ref[0, 1] + 2) * (NX // 32)).astype(F32)
    rate, drag = rates(flag, spacing)
    drag = drag[:, :LANES]

    for lev in range(LEV):
        for half in range(2):
            packed = planar_ref[2 * lev + half]
            for part in range(4):
                turned = packed if part == 0 else pltpu.roll(packed, LANES - part * FR, 1)
                for comp in range(COMP):
                    for j in range(2):
                        at = half * HALF + 4 * j + part
                        target[comp, lev, at : at + 1, :] = turned[2 * comp + j : 2 * comp + j + 1]
        first, second = target[0, lev], target[1, lev]
        aims = [cosine * first - sine * second, sine * first + cosine * second, target[2, lev]]
        for comp in range(COMP):
            pull = rate * aims[comp]
            target[comp, lev] = pull
            full[comp, lev] = pred_ref[comp, lev, :, :LANES] + pull
    for side in range(2):
        packed = jnp.concatenate([planar_ref[2 * lev + side, 6:7, :] for lev in range(LEV)], axis=0)
        aims = [packed] + [pltpu.roll(packed, LANES - comp * FR, 1) for comp in range(1, COMP)]
        aims = [cosine * aims[0] - sine * aims[1], sine * aims[0] + cosine * aims[1], aims[2]]
        for comp in range(COMP):
            edge[side, comp] = edge_ref[side, comp, :, :LANES] + rate * aims[comp]

    row = row_iota(CY, LANES)
    lane = lane_iota(CY, LANES)
    copies = []
    for lev in range(LEV):
        stream, cross = full[0, lev], full[1, lev]
        loss = rate + drag * jnp.abs(stream) if 1 <= lev <= LEV // 2 else rate
        last = 0.05 * (1.0 - pred_ref[0, lev, :, LANES:])
        for comp in range(COMP):
            u = full[comp, lev]
            right = pred_ref[comp, lev, :, LANES:]
            pull = target[comp, lev]
            below = -u if lev == 0 else full[comp, lev - 1]
            above = u if lev == LEV - 1 else full[comp, lev + 1]
            north = jnp.where(row == CY - 1, edge[1, comp, lev : lev + 1, :], pltpu.roll(u, CY - 1, 0))
            south = jnp.where(row == 0, edge[0, comp, lev : lev + 1, :], pltpu.roll(u, 1, 0))
            east = pltpu.roll(jnp.where(lane == 0, right, u), LANES - 1, 1)
            west = pltpu.roll(jnp.where(lane == LANES - 1, right, u), 1, 1)
            moved = change(u, stream, cross, west, east, north, south, above, below) + (pull - loss * u)
            result[comp, lev, :, :LANES] = 0.5 * (fields_ref[0, comp, lev, :, :LANES] + u + moved)
            passed = jnp.where(lane == LANES - 1, pltpu.roll(pull, LANES - 1, 1), 0.0)
            result[comp, lev, :, LANES:] = right_ref[comp, lev] + last * passed
        copy = pltpu.make_async_copy(result.at[:, lev], out_ref.at[0, :, lev], sems.at[lev])
        copy.start()
        copies.append(copy)
    for copy in copies:
        copy.wait()


def local(fields, sample_index, stencil, stencil_weight):
    message, low, high = pl.pallas_call(
        pack_kernel,
        out_shape=(shape(GROUPS, CY, LANES), shape(COMP, 2, LEV, NX), shape(COMP, 2, LEV, NX)),
        in_specs=[HBM, HBM],
        out_specs=(VMEM, VMEM, VMEM),
        scratch_shapes=[
            pltpu.SMEM((1, COMP), jnp.int32),
            pltpu.VMEM((COMP, LEV, CY, NX), F32),
            pltpu.SemaphoreType.DMA((7,)),
        ],
        compiler_params=params(PACK_KIB),
        name="pack",
    )(sample_index, fields)
    up = [(i, (i + 1) % TILES) for i in range(TILES)]
    down = [(j, i) for i, j in up]
    before = lax.ppermute(high, "tile", up)
    after = lax.ppermute(low, "tile", down)
    asked = lax.all_to_all(message, "group", 0, 0, tiled=True)
    base, key, weight = pl.pallas_call(
        prepare_kernel,
        out_shape=(
            shape(16, LANES, dtype=jnp.int32),
            shape(STEN, 16, LANES, dtype=jnp.int32),
            shape(STEN, 16, LANES),
        ),
        in_specs=[HBM, HBM],
        out_specs=(VMEM, VMEM, VMEM),
        scratch_shapes=[
            pltpu.VMEM((NYAW, HALF, LANES), jnp.int32),
            pltpu.VMEM((NYAW, HALF, LANES), F32),
            pltpu.VMEM((NYAW, HALF, LANES), jnp.int32),
            pltpu.VMEM((NYAW, HALF, LANES), F32),
            pltpu.VMEM((512, 512), BF16),
            pltpu.SemaphoreType.DMA((4,)),
        ],
        compiler_params=params(),
        cost_estimate=cost(2 * 80 * 512 * 512, 200_000),
        name="prepare",
    )(stencil, stencil_weight)
    band = lax.all_to_all(
        jnp.broadcast_to(asked[0:1], (TILES, CY, LANES)), "tile", 0, 0, tiled=True
    )
    pred, edge, right = pl.pallas_call(
        begin_kernel,
        out_shape=(
            shape(COMP, LEV, CY, NX),
            shape(2, COMP, LEV, NX),
            shape(COMP, LEV, CY, LANES),
        ),
        in_specs=[SMEM] + [VMEM] * 5,
        out_specs=(VMEM, VMEM, VMEM),
        compiler_params=params(),
        cost_estimate=cost(8_000_000, 1_000_000),
        name="begin",
    )(sample_index, fields, low, high, before, after)
    band, pred, edge, right = lax.optimization_barrier((band, pred, edge, right))
    answers = pl.pallas_call(
        interpolate_kernel,
        out_shape=shape(GROUPS, 8, LANES),
        in_specs=[VMEM] * 5,
        out_specs=VMEM,
        scratch_shapes=[
            pltpu.VMEM((VC * 2 * FR, 2 * NY), BF16),
            pltpu.VMEM((NYAW * NYAW, 8, LANES), F32),
            pltpu.VMEM((16, LANES), F32),
        ],
        compiler_params=params(),
        name="interpolate",
    )(band, asked, base, key, weight)
    planar = lax.all_to_all(answers, "group", 0, 0, tiled=True)
    return pl.pallas_call(
        finish_kernel,
        out_shape=shape(1, COMP, LEV, CY, NX),
        in_specs=[SMEM] + [VMEM] * 5,
        out_specs=HBM,
        scratch_shapes=[
            pltpu.VMEM((COMP, LEV, CY, LANES), F32),
            pltpu.VMEM((COMP, LEV, CY, LANES), F32),
            pltpu.VMEM((2, COMP, LEV, LANES), F32),
            pltpu.VMEM((COMP, LEV, CY, NX), F32),
            pltpu.SemaphoreType.DMA((LEV,)),
        ],
        compiler_params=params(),
        name="finish",
    )(sample_index, fields, planar, pred, edge, right)


def solution(mesh):
    in_specs = (P("group", None, None, "tile", None), P("group", None), P(), P())
    out_specs = P("group", None, None, "tile", None)
    return jax.shard_map(local, mesh=mesh, in_specs=in_specs, out_specs=out_specs, check_vma=False)
```

```python
import jax
import jax.numpy as jnp
import numpy as np
from jax import lax
from jax.experimental import pallas as pl
from jax.experimental.pallas import tpu as pltpu
from jax.sharding import PartitionSpec as P

COMP = 3
LEV = 8
CY = 16
NX = 256
FR = 32
PACK_KIB = 60000
STEN = 4
NYAW = 4
GROUPS = 16
NY = 256
TILES = NY // CY
HALF = CY // 2
LANES = 128
VC = NYAW * COMP
CELLS = 2 * NYAW + 1

TIME_STEP = 0.2
YAW_STEP = 0.2
SIGMA_PEAK = 2.5

F32 = jnp.float32
BF16 = jnp.bfloat16
VMEM = pl.BlockSpec(memory_space=pltpu.VMEM)
SMEM = pl.BlockSpec(memory_space=pltpu.SMEM)
HBM = pl.BlockSpec(memory_space=pltpu.HBM)


def params(kib=48 * 1024):
    return pltpu.CompilerParams(vmem_limit_bytes=kib * 1024)


def cost(flops, moved):
    return pl.CostEstimate(flops=flops, bytes_accessed=moved, transcendentals=0)


def shape(*dims, dtype=F32):
    return jax.ShapeDtypeStruct(dims, dtype)


def lane_iota(rows, lanes):
    return lax.broadcasted_iota(jnp.int32, (rows, lanes), 1)


def row_iota(rows, lanes):
    return lax.broadcasted_iota(jnp.int32, (rows, lanes), 0)


def pack_kernel(sample_hbm, fields_hbm, msg_ref, low_ref, high_ref, sample_ref, fields_ref, sems):
    sample_copy = pltpu.make_async_copy(sample_hbm, sample_ref, sems.at[0])
    sample_copy.start()
    halves = [pl.ds(NX - LANES, LANES), pl.ds(0, LANES)]
    copies = [
        [
            pltpu.make_async_copy(
                fields_hbm.at[comp, :, lanes], fields_ref.at[at, comp], sems.at[1 + 3 * at + comp]
            )
            for comp in range(COMP)
        ]
        for at, lanes in enumerate(halves)
    ]
    for part in copies:
        for copy in part:
            copy.start()
    for copy in copies[0]:
        copy.wait()
    sample_copy.wait()
    combo = (sample_ref[0, 2] * NYAW + sample_ref[0, 0]).astype(F32)
    lane = lane_iota(CY, LANES)
    for lev in range(LEV):
        packed = jnp.full((CY, LANES), combo, F32)
        for comp in range(COMP):
            band = pltpu.roll(fields_ref[0, comp, lev * CY : (lev + 1) * CY, :], (comp + 1) * FR, 1)
            packed = jnp.where((lane >= comp * FR) & (lane < (comp + 1) * FR), band, packed)
        msg_ref[2 * lev] = packed
        msg_ref[2 * lev + 1] = packed
    for copy in copies[1]:
        copy.wait()
    for comp in range(COMP):
        for row in range(2):
            for at, lanes in enumerate(halves):
                part = fields_ref.at[at, comp]
                low_ref[comp, row, :, lanes] = part[pl.ds(row, LEV, stride=CY), :]
                high_ref[comp, row, :, lanes] = part[pl.ds(CY - 2 + row, LEV, stride=CY), :]


def prepare_kernel(
    stencil_ref, weight_ref, hot_ref, spread_ref, sten, wts, sten_x, wts_x, perm, sems
):
    half = lax.axis_index("group") % 2
    start = lax.axis_index("tile") * CY + half * HALF
    beyond = (start + jnp.where(half == 0, NY - HALF, HALF)) % NY
    start = pl.multiple_of(start, HALF)
    beyond = pl.multiple_of(beyond, HALF)
    copies = [
        pltpu.make_async_copy(stencil_ref.at[:, pl.ds(start, HALF), :], sten, sems.at[0]),
        pltpu.make_async_copy(weight_ref.at[:, pl.ds(start, HALF), :], wts, sems.at[1]),
        pltpu.make_async_copy(stencil_ref.at[:, pl.ds(beyond, HALF), :], sten_x, sems.at[2]),
        pltpu.make_async_copy(weight_ref.at[:, pl.ds(beyond, HALF), :], wts_x, sems.at[3]),
    ]
    for copy in copies:
        copy.start()
    source = row_iota(512, 512)
    target = (source % 4) * LANES + (source // LANES) * FR + (source % LANES) // 4
    perm[...] = jnp.where(target == lane_iota(512, 512), 1.0, 0.0).astype(BF16)
    for copy in copies:
        copy.wait()

    def gathered(main, extra):
        parts = []
        for part in range(4):
            rows = [main[yaw, 2 * part : 2 * part + 2, :] for yaw in range(NYAW)]
            outer = jnp.where(half == 0, extra[part, HALF - 1 : HALF, :], extra[part, 0:1, :])
            rows.append(outer)
            rows.append(jnp.zeros((7, LANES), outer.dtype))
            parts.append(jnp.concatenate(rows, axis=0))
        return jnp.concatenate(parts, axis=1)

    index = gathered(sten, sten_x)
    weight = gathered(wts, wts_x)
    first = weight.astype(BF16)
    rest = weight - first.astype(F32)
    second = rest.astype(BF16)
    third = (rest - second.astype(F32)).astype(BF16)
    source_row = (index >> 5).astype(F32).astype(BF16)
    source_col = (index & 31).astype(F32).astype(BF16)
    stacked = jnp.concatenate([source_row, source_col, first, second, third], axis=0)
    sorted_ = jnp.dot(stacked, perm[...], preferred_element_type=F32)
    weight = (sorted_[32:48] + sorted_[48:64]) + sorted_[64:80]
    rows = [sorted_[0:16, k * LANES : (k + 1) * LANES] for k in range(STEN)]
    cols = [sorted_[16:32, k * LANES : (k + 1) * LANES] for k in range(STEN)]
    below = jnp.zeros((16, LANES), F32)
    for k in range(1, STEN):
        delta = rows[k] - rows[0]
        below = jnp.where((delta == -1.0) | (delta == NY - 1.0), 1.0, below)
    base = rows[0] - below
    base = jnp.where(base < 0.0, base + NY, base)
    keys = []
    for k in range(STEN):
        offset = rows[k] - base
        offset = jnp.where(offset < 0.0, offset + NY, offset)
        keys.append(offset * FR + cols[k])
    row_ids = row_iota(NY, LANES).astype(F32)
    key_ids = row_iota(2 * FR, LANES).astype(F32)
    for cell in range(CELLS):
        lanes = slice(cell * LANES, (cell + 1) * LANES)
        hot_ref[:, lanes] = jnp.where(row_ids == base[cell : cell + 1], 1.0, 0.0).astype(BF16)
        spread = jnp.zeros((2 * FR, LANES), F32)
        for k in range(STEN):
            share = weight[cell : cell + 1, k * LANES : (k + 1) * LANES]
            spread = spread + jnp.where(key_ids == keys[k][cell : cell + 1], share, 0.0)
        spread_ref[:, lanes] = spread


def interpolate_kernel(
    band_ref, asked_ref, hot_ref, spread_ref, out_ref, table, picked, outer
):
    level = lax.axis_index("group") // 2
    band = band_ref[...].reshape(NY, LANES).T[: COMP * FR]
    for veer in range(NYAW):
        for step in range(2):
            shift = (NY - (veer * (level + 1) * (CY // 4) + step)) % NY
            moved = band if veer + step == 0 else pltpu.roll(band, shift, 1)
            upper = moved.astype(BF16)
            lower = (moved - upper.astype(F32)).astype(BF16)
            for comp in range(COMP):
                at = ((veer * COMP + comp) * 2 + step) * FR
                table[at : at + FR, 0:NY] = upper[comp * FR : (comp + 1) * FR]
                table[at : at + FR, NY : 2 * NY] = lower[comp * FR : (comp + 1) * FR]
    for pair in range(5):
        cells = [cell for cell in (2 * pair, 2 * pair + 1) if cell < CELLS]
        ones = hot_ref[:, 2 * pair * LANES : (2 * pair + len(cells)) * LANES]
        product = jnp.dot(table[...], jnp.concatenate([ones, ones], axis=0), preferred_element_type=F32)
        for at, cell in enumerate(cells):
            weights = spread_ref[:, cell * LANES : (cell + 1) * LANES]
            for one in range(VC):
                value = jnp.sum(
                    product[one * 2 * FR : (one + 1) * 2 * FR, at * LANES : (at + 1) * LANES] * weights,
                    axis=0,
                    keepdims=True,
                )
                veer, comp = divmod(one, COMP)
                if cell < 2 * NYAW:
                    yaw, j = divmod(cell, 2)
                    picked[veer * NYAW + yaw, 4 * j + comp : 4 * j + comp + 1, :] = value
                else:
                    outer[one : one + 1, :] = value
    lane = lane_iota(1, LANES)
    rolled = [outer[...] if turn == 0 else pltpu.roll(outer[...], turn * FR, 1) for turn in range(4)]
    for veer in range(NYAW):
        for yaw in range(NYAW):
            rows = [
                rolled[(comp - yaw) % 4][veer * COMP + comp : veer * COMP + comp + 1] for comp in range(COMP)
            ]
            row = jnp.where(lane < FR, rows[0], jnp.where(lane < 2 * FR, rows[1], rows[2]))
            picked[veer * NYAW + yaw, 3:4, :] = row
            picked[veer * NYAW + yaw, 7:8, :] = row
    tile_lane = lane_iota(8, LANES)
    for group in range(GROUPS):
        asked = jnp.where(tile_lane >= COMP * FR, asked_ref[group, 0:8, :], 0.0)
        asked = asked + pltpu.roll(asked, FR, 1)
        asked = asked + pltpu.roll(asked, 2 * FR, 1)
        veer_asked = jnp.floor(asked * (1.0 / NYAW))
        yaw_asked = asked - NYAW * veer_asked
        of_yaw = [yaw_asked == float(yaw) for yaw in range(NYAW)]
        chosen = None
        for veer in range(NYAW):
            one = picked[veer * NYAW]
            for yaw in range(1, NYAW):
                one = jnp.where(of_yaw[yaw], picked[veer * NYAW + yaw], one)
            chosen = one if veer == 0 else jnp.where(veer_asked == float(veer), one, chosen)
        out_ref[group] = chosen


def rates(flag, spacing):
    column = lane_iota(1, LANES).astype(F32)
    rate = SIGMA_PEAK * 4.0 * (column + 1.0) * (FR - column) / float((FR + 1) ** 2)
    rate = jnp.where(column < FR, rate, 0.0) * flag
    column = lane_iota(CY, NX).astype(F32)
    row = row_iota(CY, NX)
    first_col = float(FR + NX // 16)
    away = column - first_col
    count = jnp.floor(away / spacing + 0.5)
    mask = (column >= first_col) & (column < NX - NX // 16) & (count * spacing == away)
    mask = mask & (row >= CY * 3 // 8) & (row < CY * 5 // 8)
    return rate, jnp.where(mask, flag, 0.0)


def change(u, stream, cross, west, east, north, south, above, below):
    total = (east + west) + (north + south) + (above + below) - 6.0 * u
    return 0.1 * (total - stream * (east - west) - cross * (north - south))


def begin_kernel(
    sample_ref, fields_ref, high_ref, low_ref, after_ref, before_ref, pred_ref, edge_ref, right_ref
):
    flag = jnp.where(lax.axis_index("group") > 0, TIME_STEP, 0.0).astype(F32)
    spacing = ((sample_ref[0, 1] + 2) * (NX // 32)).astype(F32)
    rate, drag = rates(flag, spacing)
    rate = jnp.concatenate([rate, jnp.zeros((1, LANES), F32)], axis=1)
    row = row_iota(CY, NX)

    level_ids = row_iota(LEV, NX)
    for side in range(2):
        if side == 0:
            here = [before_ref[comp, 1] for comp in range(COMP)]
            south = [before_ref[comp, 0] for comp in range(COMP)]
            north = [low_ref[comp, 0] for comp in range(COMP)]
        else:
            here = [after_ref[comp, 0] for comp in range(COMP)]
            south = [high_ref[comp, 1] for comp in range(COMP)]
            north = [after_ref[comp, 1] for comp in range(COMP)]
        for comp in range(COMP):
            u = here[comp]
            below = jnp.where(level_ids == 0, -u, pltpu.roll(u, 1, 0))
            above = jnp.where(level_ids == LEV - 1, u, pltpu.roll(u, LEV - 1, 0))
            west, east = pltpu.roll(u, 1, 1), pltpu.roll(u, NX - 1, 1)
            moved = change(u, here[0], here[1], west, east, north[comp], south[comp], above, below)
            edge_ref[side, comp] = u + moved - rate * u

    for lev in range(LEV):
        stream, cross = fields_ref[0, 0, lev], fields_ref[0, 1, lev]
        loss = rate + drag * jnp.abs(stream) if 1 <= lev <= LEV // 2 else rate
        for comp in range(COMP):
            u = fields_ref[0, comp, lev]
            below = -u if lev == 0 else fields_ref[0, comp, lev - 1]
            above = u if lev == LEV - 1 else fields_ref[0, comp, lev + 1]
            north = jnp.where(row == CY - 1, after_ref[comp, 0, lev : lev + 1, :], pltpu.roll(u, CY - 1, 0))
            south = jnp.where(row == 0, before_ref[comp, 1, lev : lev + 1, :], pltpu.roll(u, 1, 0))
            west, east = pltpu.roll(u, 1, 1), pltpu.roll(u, NX - 1, 1)
            moved = change(u, stream, cross, west, east, north, south, above, below)
            pred_ref[comp, lev] = u + moved - loss * u

    row = row_iota(CY, LANES)
    lane = lane_iota(CY, LANES)
    for lev in range(LEV):
        stream, cross = pred_ref[0, lev, :, LANES:], pred_ref[1, lev, :, LANES:]
        for comp in range(COMP):
            u = pred_ref[comp, lev, :, LANES:]
            left = pred_ref[comp, lev, :, :LANES]
            below = -u if lev == 0 else pred_ref[comp, lev - 1, :, LANES:]
            above = u if lev == LEV - 1 else pred_ref[comp, lev + 1, :, LANES:]
            north = jnp.where(row == CY - 1, edge_ref[1, comp, lev : lev + 1, LANES:], pltpu.roll(u, CY - 1, 0))
            south = jnp.where(row == 0, edge_ref[0, comp, lev : lev + 1, LANES:], pltpu.roll(u, 1, 0))
            east = pltpu.roll(jnp.where(lane == 0, left, u), LANES - 1, 1)
            west = pltpu.roll(jnp.where(lane == LANES - 1, left, u), 1, 1)
            moved = change(u, stream, cross, west, east, north, south, above, below)
            if 1 <= lev <= LEV // 2:
                moved = moved - drag[:, LANES:] * jnp.abs(stream) * u
            right_ref[comp, lev] = 0.5 * (fields_ref[0, comp, lev, :, LANES:] + u + moved)


def finish_kernel(
    sample_ref, fields_ref, planar_ref, pred_ref, edge_ref, right_ref, out_ref, unpacked, target, full, edge, result, sems
):
    flag = jnp.where(lax.axis_index("group") > 0, TIME_STEP, 0.0).astype(F32)
    yaw = sample_ref[0, 0]
    angles = np.float32(YAW_STEP) * (np.arange(NYAW, dtype=np.float32) - np.float32(1.5))
    cosine = jnp.float32(np.cos(angles[0]))
    sine = jnp.float32(np.sin(angles[0]))
    for at in range(1, NYAW):
        cosine = jnp.where(yaw == at, jnp.float32(np.cos(angles[at])), cosine)
        sine = jnp.where(yaw == at, jnp.float32(np.sin(angles[at])), sine)
    spacing = ((sample_ref[0, 1] + 2) * (NX // 32)).astype(F32)
    rate, drag = rates(flag, spacing)
    drag = drag[:, :LANES]

    for lev in range(LEV):
        for half in range(2):
            packed = planar_ref[2 * lev + half]
            for part in range(4):
                turned = packed if part == 0 else pltpu.roll(packed, LANES - part * FR, 1)
                unpacked[2 * lev + half, 8 * part : 8 * part + 8, :] = turned
        aims = [
            jnp.concatenate(
                [unpacked[2 * lev + half, pl.ds(comp, HALF, stride=4), :] for half in range(2)], axis=0
            )
            for comp in range(COMP)
        ]
        aims = [cosine * aims[0] - sine * aims[1], sine * aims[0] + cosine * aims[1], aims[2]]
        for comp in range(COMP):
            pull = rate * aims[comp]
            target[comp, lev] = pull
            full[comp, lev] = pred_ref[comp, lev, :, :LANES] + pull
    for side in range(2):
        packed = jnp.concatenate([planar_ref[2 * lev + side, 3:4, :] for lev in range(LEV)], axis=0)
        aims = [packed] + [pltpu.roll(packed, LANES - comp * FR, 1) for comp in range(1, COMP)]
        aims = [cosine * aims[0] - sine * aims[1], sine * aims[0] + cosine * aims[1], aims[2]]
        for comp in range(COMP):
            edge[side, comp] = edge_ref[side, comp, :, :LANES] + rate * aims[comp]

    row = row_iota(CY, LANES)
    lane = lane_iota(CY, LANES)
    copies = []
    for lev in range(LEV):
        stream, cross = full[0, lev], full[1, lev]
        loss = rate + drag * jnp.abs(stream) if 1 <= lev <= LEV // 2 else rate
        last = 0.05 * (1.0 - pred_ref[0, lev, :, LANES:])
        for comp in range(COMP):
            u = full[comp, lev]
            right = pred_ref[comp, lev, :, LANES:]
            pull = target[comp, lev]
            below = -u if lev == 0 else full[comp, lev - 1]
            above = u if lev == LEV - 1 else full[comp, lev + 1]
            north = jnp.where(row == CY - 1, edge[1, comp, lev : lev + 1, :], pltpu.roll(u, CY - 1, 0))
            south = jnp.where(row == 0, edge[0, comp, lev : lev + 1, :], pltpu.roll(u, 1, 0))
            east = pltpu.roll(jnp.where(lane == 0, right, u), LANES - 1, 1)
            west = pltpu.roll(jnp.where(lane == LANES - 1, right, u), 1, 1)
            moved = change(u, stream, cross, west, east, north, south, above, below) + (pull - loss * u)
            result[comp, lev, :, :LANES] = 0.5 * (fields_ref[0, comp, lev, :, :LANES] + u + moved)
            passed = jnp.where(lane == LANES - 1, pltpu.roll(pull, LANES - 1, 1), 0.0)
            result[comp, lev, :, LANES:] = right_ref[comp, lev] + last * passed
        copy = pltpu.make_async_copy(result.at[:, lev], out_ref.at[0, :, lev], sems.at[lev])
        copy.start()
        copies.append(copy)
    for copy in copies:
        copy.wait()


def local(fields, sample_index, stencil, stencil_weight):
    message, low, high = pl.pallas_call(
        pack_kernel,
        out_shape=(shape(GROUPS, CY, LANES), shape(COMP, 2, LEV, NX), shape(COMP, 2, LEV, NX)),
        in_specs=[HBM, HBM],
        out_specs=(VMEM, VMEM, VMEM),
        scratch_shapes=[
            pltpu.SMEM((1, COMP), jnp.int32),
            pltpu.VMEM((2, COMP, LEV * CY, LANES), F32),
            pltpu.SemaphoreType.DMA((7,)),
        ],
        compiler_params=params(PACK_KIB),
        name="pack",
    )(sample_index, fields.reshape(COMP, LEV * CY, NX))
    up = [(i, (i + 1) % TILES) for i in range(TILES)]
    down = [(j, i) for i, j in up]
    after = lax.ppermute(low, "tile", down)
    before = lax.ppermute(high, "tile", up)
    asked = lax.all_to_all(message, "group", 0, 0, tiled=True)
    hot, spread = pl.pallas_call(
        prepare_kernel,
        out_shape=(
            shape(NY, CELLS * LANES, dtype=BF16),
            shape(2 * FR, CELLS * LANES),
        ),
        in_specs=[HBM, HBM],
        out_specs=(VMEM, VMEM),
        scratch_shapes=[
            pltpu.VMEM((NYAW, HALF, LANES), jnp.int32),
            pltpu.VMEM((NYAW, HALF, LANES), F32),
            pltpu.VMEM((NYAW, HALF, LANES), jnp.int32),
            pltpu.VMEM((NYAW, HALF, LANES), F32),
            pltpu.VMEM((512, 512), BF16),
            pltpu.SemaphoreType.DMA((4,)),
        ],
        compiler_params=params(),
        cost_estimate=cost(100_000_000_000, 200_000),
        name="prepare",
    )(stencil, stencil_weight)
    band = lax.all_to_all(
        jnp.broadcast_to(asked[0:1], (TILES, CY, LANES)), "tile", 0, 0, tiled=True
    )
    pred, edge, right = pl.pallas_call(
        begin_kernel,
        out_shape=(
            shape(COMP, LEV, CY, NX),
            shape(2, COMP, LEV, NX),
            shape(COMP, LEV, CY, LANES),
        ),
        in_specs=[SMEM] + [VMEM] * 5,
        out_specs=(VMEM, VMEM, VMEM),
        compiler_params=params(),
        cost_estimate=cost(8_000_000, 1_000_000),
        name="begin",
    )(sample_index, fields, high, low, after, before)
    band, pred, edge, right = lax.optimization_barrier((band, pred, edge, right))
    answers = pl.pallas_call(
        interpolate_kernel,
        out_shape=shape(GROUPS, 8, LANES),
        in_specs=[VMEM] * 4,
        out_specs=VMEM,
        scratch_shapes=[
            pltpu.VMEM((VC * 2 * FR, 2 * NY), BF16),
            pltpu.VMEM((NYAW * NYAW, 8, LANES), F32),
            pltpu.VMEM((16, LANES), F32),
        ],
        compiler_params=params(),
        name="interpolate",
    )(band, asked, hot, spread)
    planar = lax.all_to_all(answers, "group", 0, 0, tiled=True)
    return pl.pallas_call(
        finish_kernel,
        out_shape=shape(1, COMP, LEV, CY, NX),
        in_specs=[SMEM] + [VMEM] * 5,
        out_specs=HBM,
        scratch_shapes=[
            pltpu.VMEM((2 * LEV, 4 * HALF, LANES), F32),
            pltpu.VMEM((COMP, LEV, CY, LANES), F32),
            pltpu.VMEM((COMP, LEV, CY, LANES), F32),
            pltpu.VMEM((2, COMP, LEV, LANES), F32),
            pltpu.VMEM((COMP, LEV, CY, NX), F32),
            pltpu.SemaphoreType.DMA((LEV,)),
        ],
        compiler_params=params(),
        name="finish",
    )(sample_index, fields, planar, pred, edge, right)


def solution(mesh):
    in_specs = (P("group", None, None, "tile", None), P("group", None), P(), P())
    out_specs = P("group", None, None, "tile", None)
    return jax.shard_map(local, mesh=mesh, in_specs=in_specs, out_specs=out_specs, check_vma=False)
```

```python
import jax
import jax.numpy as jnp
import numpy as np
from jax import lax
from jax.experimental import pallas as pl
from jax.experimental.pallas import tpu as pltpu
from jax.sharding import PartitionSpec as P

COMP = 3
LEV = 8
CY = 16
NX = 256
FR = 32
PACK_KIB = 60000
STEN = 4
NYAW = 4
GROUPS = 16
NY = 256
TILES = NY // CY
HALF = CY // 2
LANES = 128
CELLS = 2 * NYAW + 1

TIME_STEP = 0.2
YAW_STEP = 0.2
SIGMA_PEAK = 2.5

F32 = jnp.float32
BF16 = jnp.bfloat16
VMEM = pl.BlockSpec(memory_space=pltpu.VMEM)
SMEM = pl.BlockSpec(memory_space=pltpu.SMEM)
HBM = pl.BlockSpec(memory_space=pltpu.HBM)


def params(kib=48 * 1024):
    return pltpu.CompilerParams(vmem_limit_bytes=kib * 1024)


def cost(flops, moved):
    return pl.CostEstimate(flops=flops, bytes_accessed=moved, transcendentals=0)


def shape(*dims, dtype=F32):
    return jax.ShapeDtypeStruct(dims, dtype)


def lane_iota(rows, lanes):
    return lax.broadcasted_iota(jnp.int32, (rows, lanes), 1)


def row_iota(rows, lanes):
    return lax.broadcasted_iota(jnp.int32, (rows, lanes), 0)


def pack_kernel(sample_hbm, fields_hbm, msg_ref, low_ref, high_ref, sample_ref, fields_ref, sems):
    sample_copy = pltpu.make_async_copy(sample_hbm, sample_ref, sems.at[0])
    sample_copy.start()
    halves = [pl.ds(NX - LANES, LANES), pl.ds(0, LANES)]
    copies = [
        [
            pltpu.make_async_copy(
                fields_hbm.at[comp, :, lanes], fields_ref.at[at, comp], sems.at[1 + 3 * at + comp]
            )
            for comp in range(COMP)
        ]
        for at, lanes in enumerate(halves)
    ]
    for part in copies:
        for copy in part:
            copy.start()
    for copy in copies[0]:
        copy.wait()
    sample_copy.wait()
    combo = (sample_ref[0, 2] * NYAW + sample_ref[0, 0]).astype(F32)
    lane = lane_iota(HALF, LANES)
    for lev in range(LEV):
        bands = [fields_ref[0, comp, lev * CY : (lev + 1) * CY, :] for comp in range(COMP)]
        for at in range(2):
            packed = pltpu.roll(bands[at][:HALF], FR, 1)
            packed = jnp.where(lane < FR, packed, pltpu.roll(bands[2][:HALF], 2 * FR, 1))
            packed = jnp.where(lane < 2 * FR, packed, pltpu.roll(bands[at][HALF:], 3 * FR, 1))
            packed = jnp.where(lane < 3 * FR, packed, bands[2][HALF:])
            msg_ref[2 * lev + at, 0:HALF, :] = packed
            msg_ref[2 * lev + at, HALF:CY, :] = jnp.full((HALF, LANES), combo, F32)
    for copy in copies[1]:
        copy.wait()
    for comp in range(COMP):
        for row in range(2):
            for at, lanes in enumerate(halves):
                part = fields_ref.at[at, comp]
                low_ref[comp, row, :, lanes] = part[pl.ds(row, LEV, stride=CY), :]
                high_ref[comp, row, :, lanes] = part[pl.ds(CY - 2 + row, LEV, stride=CY), :]


def prepare_kernel(
    stencil_ref, weight_ref, hot_ref, spread_ref, sten, wts, sten_x, wts_x, perm, sems
):
    halves = [lax.axis_index("group") % 2, 1 - lax.axis_index("group") % 2]
    copies = []
    for slot, half in enumerate(halves):
        start = lax.axis_index("tile") * CY + half * HALF
        beyond = (start + jnp.where(half == 0, NY - HALF, HALF)) % NY
        start = pl.multiple_of(start, HALF)
        beyond = pl.multiple_of(beyond, HALF)
        copies += [
            pltpu.make_async_copy(stencil_ref.at[:, pl.ds(start, HALF), :], sten.at[slot], sems.at[slot, 0]),
            pltpu.make_async_copy(weight_ref.at[:, pl.ds(start, HALF), :], wts.at[slot], sems.at[slot, 1]),
            pltpu.make_async_copy(stencil_ref.at[:, pl.ds(beyond, HALF), :], sten_x.at[slot], sems.at[slot, 2]),
            pltpu.make_async_copy(weight_ref.at[:, pl.ds(beyond, HALF), :], wts_x.at[slot], sems.at[slot, 3]),
        ]
    for copy in copies:
        copy.start()
    source = row_iota(512, 512)
    target = (source % 4) * LANES + (source // LANES) * FR + (source % LANES) // 4
    perm[...] = jnp.where(target == lane_iota(512, 512), 1.0, 0.0).astype(BF16)
    for copy in copies:
        copy.wait()

    def gathered(main, extra):
        parts = []
        for part in range(4):
            rows = []
            for slot, half in enumerate(halves):
                rows += [main[slot, yaw, 2 * part : 2 * part + 2, :] for yaw in range(NYAW)]
                outer = jnp.where(
                    half == 0, extra[slot, part, HALF - 1 : HALF, :], extra[slot, part, 0:1, :]
                )
                rows.append(outer)
                rows.append(jnp.zeros((7, LANES), outer.dtype))
            parts.append(jnp.concatenate(rows, axis=0))
        return jnp.concatenate(parts, axis=1)

    index = gathered(sten, sten_x)
    weight = gathered(wts, wts_x)
    first = weight.astype(BF16)
    rest = weight - first.astype(F32)
    second = rest.astype(BF16)
    third = (rest - second.astype(F32)).astype(BF16)
    source_row = (index >> 5).astype(F32).astype(BF16)
    source_col = (index & 31).astype(F32).astype(BF16)
    stacked = jnp.concatenate([source_row, source_col, first, second, third], axis=0)
    sorted_ = jnp.dot(stacked, perm[...], preferred_element_type=F32)
    weight = (sorted_[64:96] + sorted_[96:128]) + sorted_[128:160]
    rows = [sorted_[0:32, k * LANES : (k + 1) * LANES] for k in range(STEN)]
    cols = [sorted_[32:64, k * LANES : (k + 1) * LANES] for k in range(STEN)]
    below = jnp.zeros((32, LANES), F32)
    for k in range(1, STEN):
        delta = rows[k] - rows[0]
        below = jnp.where((delta == -1.0) | (delta == NY - 1.0), 1.0, below)
    base = rows[0] - below
    base = jnp.where(base < 0.0, base + NY, base)
    keys = []
    for k in range(STEN):
        offset = rows[k] - base
        offset = jnp.where(offset < 0.0, offset + NY, offset)
        keys.append(offset * FR + cols[k])
    row_ids = row_iota(NY, LANES).astype(F32)
    key_ids = row_iota(2 * FR, LANES).astype(F32)
    for cell in range(2 * CELLS):
        at = 16 * (cell // CELLS) + cell % CELLS
        lanes = slice(cell * LANES, (cell + 1) * LANES)
        hot_ref[:, lanes] = jnp.where(row_ids == base[at : at + 1], 1.0, 0.0).astype(BF16)
        spread = jnp.zeros((2 * FR, LANES), F32)
        for k in range(STEN):
            share = weight[at : at + 1, k * LANES : (k + 1) * LANES]
            spread = spread + jnp.where(key_ids == keys[k][at : at + 1], share, 0.0)
        spread_ref[:, lanes] = spread


def interpolate_kernel(
    band_ref, asked_ref, hot_ref, spread_ref, out_ref, table, picked, outer
):
    level = lax.axis_index("group") // 2
    blocks = []
    for tile in range(TILES):
        block = band_ref[tile]
        blocks += [block, pltpu.roll(block, 2 * FR, 1)]
    band = jnp.concatenate(blocks, axis=0).T[: 2 * FR]
    rows = NYAW * 2 * FR
    for veer in range(NYAW):
        for step in range(2):
            shift = (NY - (veer * (level + 1) * (CY // 4) + step)) % NY
            moved = band if veer + step == 0 else pltpu.roll(band, shift, 1)
            upper = moved.astype(BF16)
            lower = (moved - upper.astype(F32)).astype(BF16)
            for plane in range(2):
                at = plane * rows + (veer * 2 + step) * FR
                table[at : at + FR, 0:NY] = upper[plane * FR : (plane + 1) * FR]
                table[at : at + FR, NY : 2 * NY] = lower[plane * FR : (plane + 1) * FR]
    for slot in range(2):
        planes = 2 - slot
        for pair in range(5):
            cells = [cell for cell in (2 * pair, 2 * pair + 1) if cell < CELLS]
            first = slot * CELLS + 2 * pair
            ones = hot_ref[:, first * LANES : (first + len(cells)) * LANES]
            product = jnp.dot(
                table[0 : planes * rows], jnp.concatenate([ones, ones], axis=0), preferred_element_type=F32
            )
            for at, cell in enumerate(cells):
                weights = spread_ref[:, (first + at) * LANES : (first + at + 1) * LANES]
                for plane in range(planes):
                    kind = 2 if plane == 1 else slot
                    for veer in range(NYAW):
                        top = plane * rows + veer * 2 * FR
                        value = jnp.sum(
                            product[top : top + 2 * FR, at * LANES : (at + 1) * LANES] * weights,
                            axis=0,
                            keepdims=True,
                        )
                        if cell < 2 * NYAW:
                            yaw, j = divmod(cell, 2)
                            picked[veer * NYAW + yaw, 4 * j + kind : 4 * j + kind + 1, :] = value
                        else:
                            outer[veer * COMP + kind : veer * COMP + kind + 1, :] = value
    lane = lane_iota(1, LANES)
    rolled = [outer[...] if turn == 0 else pltpu.roll(outer[...], turn * FR, 1) for turn in range(4)]
    for veer in range(NYAW):
        for yaw in range(NYAW):
            rows = [
                rolled[(comp - yaw) % 4][veer * COMP + comp : veer * COMP + comp + 1] for comp in range(COMP)
            ]
            row = jnp.where(lane < FR, rows[0], jnp.where(lane < 2 * FR, rows[1], rows[2]))
            picked[veer * NYAW + yaw, 3:4, :] = row
            picked[veer * NYAW + yaw, 7:8, :] = row
    for group in range(GROUPS):
        asked = asked_ref[group, HALF:CY, :]
        veer_asked = jnp.floor(asked * (1.0 / NYAW))
        yaw_asked = asked - NYAW * veer_asked
        of_yaw = [yaw_asked == float(yaw) for yaw in range(NYAW)]
        chosen = None
        for veer in range(NYAW):
            one = picked[veer * NYAW]
            for yaw in range(1, NYAW):
                one = jnp.where(of_yaw[yaw], picked[veer * NYAW + yaw], one)
            chosen = one if veer == 0 else jnp.where(veer_asked == float(veer), one, chosen)
        out_ref[group] = chosen


def rates(flag, spacing):
    column = lane_iota(1, LANES).astype(F32)
    rate = SIGMA_PEAK * 4.0 * (column + 1.0) * (FR - column) / float((FR + 1) ** 2)
    rate = jnp.where(column < FR, rate, 0.0) * flag
    column = lane_iota(CY, NX).astype(F32)
    row = row_iota(CY, NX)
    first_col = float(FR + NX // 16)
    away = column - first_col
    count = jnp.floor(away / spacing + 0.5)
    mask = (column >= first_col) & (column < NX - NX // 16) & (count * spacing == away)
    mask = mask & (row >= CY * 3 // 8) & (row < CY * 5 // 8)
    return rate, jnp.where(mask, flag, 0.0)


def change(u, stream, cross, west, east, north, south, above, below):
    total = (east + west) + (north + south) + (above + below) - 6.0 * u
    return 0.1 * (total - stream * (east - west) - cross * (north - south))


def begin_kernel(
    sample_ref, fields_ref, high_ref, low_ref, after_ref, before_ref, pred_ref, edge_ref, right_ref, const_ref
):
    flag = jnp.where(lax.axis_index("group") > 0, TIME_STEP, 0.0).astype(F32)
    spacing = ((sample_ref[0, 1] + 2) * (NX // 32)).astype(F32)
    rate, drag = rates(flag, spacing)
    yaw = sample_ref[0, 0]
    angles = np.float32(YAW_STEP) * (np.arange(NYAW, dtype=np.float32) - np.float32(1.5))
    cosine = jnp.float32(np.cos(angles[0]))
    sine = jnp.float32(np.sin(angles[0]))
    for at in range(1, NYAW):
        cosine = jnp.where(yaw == at, jnp.float32(np.cos(angles[at])), cosine)
        sine = jnp.where(yaw == at, jnp.float32(np.sin(angles[at])), sine)
    const_ref[0:CY, :] = drag[:, :LANES]
    const_ref[CY : CY + 1, :] = rate
    const_ref[CY + 1 : CY + 2, :] = jnp.full((1, LANES), cosine, F32)
    const_ref[CY + 2 : CY + 3, :] = jnp.full((1, LANES), sine, F32)
    const_ref[CY + 3 : CY + 8, :] = jnp.zeros((5, LANES), F32)
    rate = jnp.concatenate([rate, jnp.zeros((1, LANES), F32)], axis=1)
    row = row_iota(CY, NX)

    level_ids = row_iota(LEV, NX)
    for side in range(2):
        if side == 0:
            here = [before_ref[comp, 1] for comp in range(COMP)]
            south = [before_ref[comp, 0] for comp in range(COMP)]
            north = [low_ref[comp, 0] for comp in range(COMP)]
        else:
            here = [after_ref[comp, 0] for comp in range(COMP)]
            south = [high_ref[comp, 1] for comp in range(COMP)]
            north = [after_ref[comp, 1] for comp in range(COMP)]
        for comp in range(COMP):
            u = here[comp]
            below = jnp.where(level_ids == 0, -u, pltpu.roll(u, 1, 0))
            above = jnp.where(level_ids == LEV - 1, u, pltpu.roll(u, LEV - 1, 0))
            west, east = pltpu.roll(u, 1, 1), pltpu.roll(u, NX - 1, 1)
            moved = change(u, here[0], here[1], west, east, north[comp], south[comp], above, below)
            edge_ref[side, comp] = u + moved - rate * u

    for lev in range(LEV):
        stream, cross = fields_ref[0, 0, lev], fields_ref[0, 1, lev]
        loss = rate + drag * jnp.abs(stream) if 1 <= lev <= LEV // 2 else rate
        for comp in range(COMP):
            u = fields_ref[0, comp, lev]
            below = -u if lev == 0 else fields_ref[0, comp, lev - 1]
            above = u if lev == LEV - 1 else fields_ref[0, comp, lev + 1]
            north = jnp.where(row == CY - 1, after_ref[comp, 0, lev : lev + 1, :], pltpu.roll(u, CY - 1, 0))
            south = jnp.where(row == 0, before_ref[comp, 1, lev : lev + 1, :], pltpu.roll(u, 1, 0))
            west, east = pltpu.roll(u, 1, 1), pltpu.roll(u, NX - 1, 1)
            moved = change(u, stream, cross, west, east, north, south, above, below)
            pred_ref[comp, lev] = u + moved - loss * u

    row = row_iota(CY, LANES)
    lane = lane_iota(CY, LANES)
    for lev in range(LEV):
        stream, cross = pred_ref[0, lev, :, LANES:], pred_ref[1, lev, :, LANES:]
        for comp in range(COMP):
            u = pred_ref[comp, lev, :, LANES:]
            left = pred_ref[comp, lev, :, :LANES]
            below = -u if lev == 0 else pred_ref[comp, lev - 1, :, LANES:]
            above = u if lev == LEV - 1 else pred_ref[comp, lev + 1, :, LANES:]
            north = jnp.where(row == CY - 1, edge_ref[1, comp, lev : lev + 1, LANES:], pltpu.roll(u, CY - 1, 0))
            south = jnp.where(row == 0, edge_ref[0, comp, lev : lev + 1, LANES:], pltpu.roll(u, 1, 0))
            east = pltpu.roll(jnp.where(lane == 0, left, u), LANES - 1, 1)
            west = pltpu.roll(jnp.where(lane == LANES - 1, left, u), 1, 1)
            moved = change(u, stream, cross, west, east, north, south, above, below)
            if 1 <= lev <= LEV // 2:
                moved = moved - drag[:, LANES:] * jnp.abs(stream) * u
            right_ref[comp, lev] = 0.5 * (fields_ref[0, comp, lev, :, LANES:] + u + moved)


def finish_kernel(
    const_ref, fields_ref, planar_ref, pred_ref, edge_ref, right_ref, out_ref, unpacked, target, full, edge, result, sems
):
    drag = const_ref[0:CY, :]
    rate = const_ref[CY : CY + 1, :]
    cosine = const_ref[CY + 1 : CY + 2, :]
    sine = const_ref[CY + 2 : CY + 3, :]

    for lev in range(LEV):
        for half in range(2):
            packed = planar_ref[2 * lev + half]
            for part in range(4):
                turned = packed if part == 0 else pltpu.roll(packed, LANES - part * FR, 1)
                unpacked[2 * lev + half, 8 * part : 8 * part + 8, :] = turned
        aims = []
        for comp in range(COMP):
            parts = []
            for half in range(2):
                origin = comp if comp < 2 else half
                kind = 2 if comp == 2 else (half + comp) % 2
                parts.append(unpacked[2 * lev + origin, pl.ds(kind, HALF, stride=4), :])
            aims.append(jnp.concatenate(parts, axis=0))
        aims = [cosine * aims[0] - sine * aims[1], sine * aims[0] + cosine * aims[1], aims[2]]
        for comp in range(COMP):
            pull = rate * aims[comp]
            target[comp, lev] = pull
            full[comp, lev] = pred_ref[comp, lev, :, :LANES] + pull
    outer = [
        jnp.concatenate([planar_ref[2 * lev + at, 3:4, :] for lev in range(LEV)], axis=0) for at in range(2)
    ]
    for side in range(2):
        aims = []
        for comp in range(COMP):
            origin = comp if comp < 2 else side
            kind = 2 if comp == 2 else (side + comp) % 2
            packed = outer[origin]
            aims.append(packed if kind == 0 else pltpu.roll(packed, LANES - kind * FR, 1))
        aims = [cosine * aims[0] - sine * aims[1], sine * aims[0] + cosine * aims[1], aims[2]]
        for comp in range(COMP):
            edge[side, comp] = edge_ref[side, comp, :, :LANES] + rate * aims[comp]

    row = row_iota(CY, LANES)
    lane = lane_iota(CY, LANES)
    copies = []
    for lev in range(LEV):
        stream, cross = full[0, lev], full[1, lev]
        loss = rate + drag * jnp.abs(stream) if 1 <= lev <= LEV // 2 else rate
        last = 0.05 * (1.0 - pred_ref[0, lev, :, LANES:])
        for comp in range(COMP):
            u = full[comp, lev]
            right = pred_ref[comp, lev, :, LANES:]
            pull = target[comp, lev]
            below = -u if lev == 0 else full[comp, lev - 1]
            above = u if lev == LEV - 1 else full[comp, lev + 1]
            north = jnp.where(row == CY - 1, edge[1, comp, lev : lev + 1, :], pltpu.roll(u, CY - 1, 0))
            south = jnp.where(row == 0, edge[0, comp, lev : lev + 1, :], pltpu.roll(u, 1, 0))
            east = pltpu.roll(jnp.where(lane == 0, right, u), LANES - 1, 1)
            west = pltpu.roll(jnp.where(lane == LANES - 1, right, u), 1, 1)
            moved = change(u, stream, cross, west, east, north, south, above, below) + (pull - loss * u)
            result[comp, lev, :, :LANES] = 0.5 * (fields_ref[0, comp, lev, :, :LANES] + u + moved)
            passed = jnp.where(lane == LANES - 1, pltpu.roll(pull, LANES - 1, 1), 0.0)
            result[comp, lev, :, LANES:] = right_ref[comp, lev] + last * passed
        copy = pltpu.make_async_copy(result.at[:, lev], out_ref.at[0, :, lev], sems.at[lev])
        copy.start()
        copies.append(copy)
    for copy in copies:
        copy.wait()


def local(fields, sample_index, stencil, stencil_weight):
    message, low, high = pl.pallas_call(
        pack_kernel,
        out_shape=(shape(GROUPS, CY, LANES), shape(COMP, 2, LEV, NX), shape(COMP, 2, LEV, NX)),
        in_specs=[HBM, HBM],
        out_specs=(VMEM, VMEM, VMEM),
        scratch_shapes=[
            pltpu.SMEM((1, COMP), jnp.int32),
            pltpu.VMEM((2, COMP, LEV * CY, LANES), F32),
            pltpu.SemaphoreType.DMA((7,)),
        ],
        compiler_params=params(PACK_KIB),
        name="pack",
    )(sample_index, fields.reshape(COMP, LEV * CY, NX))
    up = [(i, (i + 1) % TILES) for i in range(TILES)]
    down = [(j, i) for i, j in up]
    after = lax.ppermute(low, "tile", down)
    before = lax.ppermute(high, "tile", up)
    asked = lax.all_to_all(message, "group", 0, 0, tiled=True)
    hot, spread = pl.pallas_call(
        prepare_kernel,
        out_shape=(
            shape(NY, 2 * CELLS * LANES, dtype=BF16),
            shape(2 * FR, 2 * CELLS * LANES),
        ),
        in_specs=[HBM, HBM],
        out_specs=(VMEM, VMEM),
        scratch_shapes=[
            pltpu.VMEM((2, NYAW, HALF, LANES), jnp.int32),
            pltpu.VMEM((2, NYAW, HALF, LANES), F32),
            pltpu.VMEM((2, NYAW, HALF, LANES), jnp.int32),
            pltpu.VMEM((2, NYAW, HALF, LANES), F32),
            pltpu.VMEM((512, 512), BF16),
            pltpu.SemaphoreType.DMA((2, 4)),
        ],
        compiler_params=params(),
        cost_estimate=cost(100_000_000_000, 200_000),
        name="prepare",
    )(stencil, stencil_weight)
    band = lax.all_to_all(
        jnp.broadcast_to(asked[0:1, :HALF], (TILES, HALF, LANES)), "tile", 0, 0, tiled=True
    )
    pred, edge, right, const = pl.pallas_call(
        begin_kernel,
        out_shape=(
            shape(COMP, LEV, CY, NX),
            shape(2, COMP, LEV, NX),
            shape(COMP, LEV, CY, LANES),
            shape(CY + 8, LANES),
        ),
        in_specs=[SMEM] + [VMEM] * 5,
        out_specs=(VMEM, VMEM, VMEM, VMEM),
        compiler_params=params(),
        cost_estimate=cost(8_000_000, 1_000_000),
        name="begin",
    )(sample_index, fields, high, low, after, before)
    band, pred, edge, right, const = lax.optimization_barrier((band, pred, edge, right, const))
    answers = pl.pallas_call(
        interpolate_kernel,
        out_shape=shape(GROUPS, 8, LANES),
        in_specs=[VMEM] * 4,
        out_specs=VMEM,
        scratch_shapes=[
            pltpu.VMEM((NYAW * 4 * FR, 2 * NY), BF16),
            pltpu.VMEM((NYAW * NYAW, 8, LANES), F32),
            pltpu.VMEM((16, LANES), F32),
        ],
        compiler_params=params(),
        name="interpolate",
    )(band, asked, hot, spread)
    planar = lax.all_to_all(answers, "group", 0, 0, tiled=True)
    return pl.pallas_call(
        finish_kernel,
        out_shape=shape(1, COMP, LEV, CY, NX),
        in_specs=[VMEM] * 6,
        out_specs=HBM,
        scratch_shapes=[
            pltpu.VMEM((2 * LEV, 4 * HALF, LANES), F32),
            pltpu.VMEM((COMP, LEV, CY, LANES), F32),
            pltpu.VMEM((COMP, LEV, CY, LANES), F32),
            pltpu.VMEM((2, COMP, LEV, LANES), F32),
            pltpu.VMEM((COMP, LEV, CY, NX), F32),
            pltpu.SemaphoreType.DMA((LEV,)),
        ],
        compiler_params=params(),
        name="finish",
    )(const, fields, planar, pred, edge, right)


def solution(mesh):
    in_specs = (P("group", None, None, "tile", None), P("group", None), P(), P())
    out_specs = P("group", None, None, "tile", None)
    return jax.shard_map(local, mesh=mesh, in_specs=in_specs, out_specs=out_specs, check_vma=False)
```

```python
import jax
import jax.numpy as jnp
import numpy as np
from jax import lax
from jax.experimental import pallas as pl
from jax.experimental.pallas import tpu as pltpu
from jax.sharding import PartitionSpec as P

COMP = 3
LEV = 8
CY = 16
NX = 256
FR = 32
PACK_KIB = 60000
STEN = 4
NYAW = 4
GROUPS = 16
NY = 256
TILES = NY // CY
TILE_ORDER = [(tile + 11) % TILES for tile in range(TILES)]
HALF = CY // 2
LANES = 128
CELLS = 2 * NYAW + 1

TIME_STEP = 0.2
YAW_STEP = 0.2
SIGMA_PEAK = 2.5

F32 = jnp.float32
BF16 = jnp.bfloat16
VMEM = pl.BlockSpec(memory_space=pltpu.VMEM)
SMEM = pl.BlockSpec(memory_space=pltpu.SMEM)
HBM = pl.BlockSpec(memory_space=pltpu.HBM)


def params(kib=48 * 1024):
    return pltpu.CompilerParams(vmem_limit_bytes=kib * 1024)


def cost(flops, moved):
    return pl.CostEstimate(flops=flops, bytes_accessed=moved, transcendentals=0)


def shape(*dims, dtype=F32):
    return jax.ShapeDtypeStruct(dims, dtype)


def lane_iota(rows, lanes):
    return lax.broadcasted_iota(jnp.int32, (rows, lanes), 1)


def row_iota(rows, lanes):
    return lax.broadcasted_iota(jnp.int32, (rows, lanes), 0)


def pack_kernel(sample_hbm, fields_hbm, msg_ref, low_ref, high_ref, sample_ref, fields_ref, sems):
    sample_copy = pltpu.make_async_copy(sample_hbm, sample_ref, sems.at[0])
    sample_copy.start()
    halves = [pl.ds(NX - LANES, LANES), pl.ds(0, LANES)]
    copies = [
        [
            pltpu.make_async_copy(
                fields_hbm.at[comp, :, lanes], fields_ref.at[at, comp], sems.at[1 + 3 * at + comp]
            )
            for comp in range(COMP)
        ]
        for at, lanes in enumerate(halves)
    ]
    for part in copies:
        for copy in part:
            copy.start()
    for copy in copies[0]:
        copy.wait()
    sample_copy.wait()
    combo = (sample_ref[0, 2] * NYAW + sample_ref[0, 0]).astype(F32)
    lane = lane_iota(HALF, LANES)
    for lev in range(LEV):
        bands = [fields_ref[0, comp, lev * CY : (lev + 1) * CY, :] for comp in range(COMP)]
        for at in range(2):
            packed = pltpu.roll(bands[at][:HALF], FR, 1)
            packed = jnp.where(lane < FR, packed, pltpu.roll(bands[2][:HALF], 2 * FR, 1))
            packed = jnp.where(lane < 2 * FR, packed, pltpu.roll(bands[at][HALF:], 3 * FR, 1))
            packed = jnp.where(lane < 3 * FR, packed, bands[2][HALF:])
            msg_ref[2 * lev + at, 0:HALF, :] = packed
            msg_ref[2 * lev + at, HALF:CY, :] = jnp.full((HALF, LANES), combo, F32)
    for copy in copies[1]:
        copy.wait()
    for comp in range(COMP):
        for row in range(2):
            for at, lanes in enumerate(halves):
                part = fields_ref.at[at, comp]
                low_ref[comp, row, :, lanes] = part[pl.ds(row, LEV, stride=CY), :]
                high_ref[comp, row, :, lanes] = part[pl.ds(CY - 2 + row, LEV, stride=CY), :]


def prepare_kernel(
    stencil_ref, weight_ref, hot_ref, spread_ref, sten, wts, sten_x, wts_x, perm, sems
):
    halves = [lax.axis_index("group") % 2, 1 - lax.axis_index("group") % 2]
    copies = []
    for slot, half in enumerate(halves):
        start = lax.axis_index("tile") * CY + half * HALF
        beyond = (start + jnp.where(half == 0, NY - HALF, HALF)) % NY
        start = pl.multiple_of(start, HALF)
        beyond = pl.multiple_of(beyond, HALF)
        copies += [
            pltpu.make_async_copy(stencil_ref.at[:, pl.ds(start, HALF), :], sten.at[slot], sems.at[slot, 0]),
            pltpu.make_async_copy(weight_ref.at[:, pl.ds(start, HALF), :], wts.at[slot], sems.at[slot, 1]),
            pltpu.make_async_copy(stencil_ref.at[:, pl.ds(beyond, HALF), :], sten_x.at[slot], sems.at[slot, 2]),
            pltpu.make_async_copy(weight_ref.at[:, pl.ds(beyond, HALF), :], wts_x.at[slot], sems.at[slot, 3]),
        ]
    for copy in copies:
        copy.start()
    source = row_iota(512, 512)
    target = (source % 4) * LANES + (source // LANES) * FR + (source % LANES) // 4
    perm[...] = jnp.where(target == lane_iota(512, 512), 1.0, 0.0).astype(BF16)
    for copy in copies:
        copy.wait()

    def gathered(main, extra):
        parts = []
        for part in range(4):
            rows = []
            for slot, half in enumerate(halves):
                rows += [main[slot, yaw, 2 * part : 2 * part + 2, :] for yaw in range(NYAW)]
                outer = jnp.where(
                    half == 0, extra[slot, part, HALF - 1 : HALF, :], extra[slot, part, 0:1, :]
                )
                rows.append(outer)
                rows.append(jnp.zeros((7, LANES), outer.dtype))
            parts.append(jnp.concatenate(rows, axis=0))
        return jnp.concatenate(parts, axis=1)

    index = gathered(sten, sten_x)
    weight = gathered(wts, wts_x)
    first = weight.astype(BF16)
    rest = weight - first.astype(F32)
    second = rest.astype(BF16)
    third = (rest - second.astype(F32)).astype(BF16)
    source_row = (index >> 5).astype(F32).astype(BF16)
    source_col = (index & 31).astype(F32).astype(BF16)
    stacked = jnp.concatenate([source_row, source_col, first, second, third], axis=0)
    sorted_ = jnp.dot(stacked, perm[...], preferred_element_type=F32)
    weight = (sorted_[64:96] + sorted_[96:128]) + sorted_[128:160]
    rows = [sorted_[0:32, k * LANES : (k + 1) * LANES] for k in range(STEN)]
    cols = [sorted_[32:64, k * LANES : (k + 1) * LANES] for k in range(STEN)]
    below = jnp.zeros((32, LANES), F32)
    for k in range(1, STEN):
        delta = rows[k] - rows[0]
        below = jnp.where((delta == -1.0) | (delta == NY - 1.0), 1.0, below)
    base = rows[0] - below
    base = jnp.where(base < 0.0, base + NY, base)
    keys = []
    for k in range(STEN):
        offset = rows[k] - base
        offset = jnp.where(offset < 0.0, offset + NY, offset)
        keys.append(offset * FR + cols[k])
    row_ids = row_iota(NY, LANES).astype(F32)
    key_ids = row_iota(2 * FR, LANES).astype(F32)
    for cell in range(2 * CELLS):
        at = 16 * (cell // CELLS) + cell % CELLS
        lanes = slice(cell * LANES, (cell + 1) * LANES)
        hot_ref[:, lanes] = jnp.where(row_ids == base[at : at + 1], 1.0, 0.0).astype(BF16)
        spread = jnp.zeros((2 * FR, LANES), F32)
        for k in range(STEN):
            share = weight[at : at + 1, k * LANES : (k + 1) * LANES]
            spread = spread + jnp.where(key_ids == keys[k][at : at + 1], share, 0.0)
        spread_ref[:, lanes] = spread


def interpolate_kernel(
    band_ref, asked_ref, hot_ref, spread_ref, out_ref, table, picked, outer
):
    level = lax.axis_index("group") // 2
    blocks = []
    for tile in range(TILES):
        block = band_ref[TILE_ORDER.index(tile)]
        blocks += [block, pltpu.roll(block, 2 * FR, 1)]
    band = jnp.concatenate(blocks, axis=0).T[: 2 * FR]
    rows = NYAW * 2 * FR
    for veer in range(NYAW):
        for step in range(2):
            shift = (NY - (veer * (level + 1) * (CY // 4) + step)) % NY
            moved = band if veer + step == 0 else pltpu.roll(band, shift, 1)
            upper = moved.astype(BF16)
            lower = (moved - upper.astype(F32)).astype(BF16)
            for plane in range(2):
                at = 2 * plane * rows + (veer * 2 + step) * FR
                table[at : at + FR, :] = upper[plane * FR : (plane + 1) * FR]
                table[at + rows : at + rows + FR, :] = lower[plane * FR : (plane + 1) * FR]
    for slot in range(2):
        planes = 2 - slot
        for pair in range(5):
            cells = [cell for cell in (2 * pair, 2 * pair + 1) if cell < CELLS]
            first = slot * CELLS + 2 * pair
            ones = hot_ref[:, first * LANES : (first + len(cells)) * LANES]
            product = jnp.dot(table[0 : 2 * planes * rows], ones, preferred_element_type=F32)
            for at, cell in enumerate(cells):
                weights = spread_ref[:, (first + at) * LANES : (first + at + 1) * LANES]
                for plane in range(planes):
                    kind = 2 if plane == 1 else slot
                    for veer in range(NYAW):
                        top = 2 * plane * rows + veer * 2 * FR
                        span = slice(at * LANES, (at + 1) * LANES)
                        upper = product[top : top + 2 * FR, span]
                        lower = product[top + rows : top + rows + 2 * FR, span]
                        value = jnp.sum((upper + lower) * weights, axis=0, keepdims=True)
                        if cell < 2 * NYAW:
                            yaw, j = divmod(cell, 2)
                            picked[veer * NYAW + yaw, 4 * j + kind : 4 * j + kind + 1, :] = value
                        else:
                            outer[veer * COMP + kind : veer * COMP + kind + 1, :] = value
    lane = lane_iota(1, LANES)
    rolled = [outer[...] if turn == 0 else pltpu.roll(outer[...], turn * FR, 1) for turn in range(4)]
    for veer in range(NYAW):
        for yaw in range(NYAW):
            rows = [
                rolled[(comp - yaw) % 4][veer * COMP + comp : veer * COMP + comp + 1] for comp in range(COMP)
            ]
            row = jnp.where(lane < FR, rows[0], jnp.where(lane < 2 * FR, rows[1], rows[2]))
            picked[veer * NYAW + yaw, 3:4, :] = row
            picked[veer * NYAW + yaw, 7:8, :] = row
    for group in range(GROUPS):
        asked = asked_ref[group, HALF:CY, :]
        veer_asked = jnp.floor(asked * (1.0 / NYAW))
        yaw_asked = asked - NYAW * veer_asked
        of_yaw = [yaw_asked == float(yaw) for yaw in range(NYAW)]
        chosen = None
        for veer in range(NYAW):
            one = picked[veer * NYAW]
            for yaw in range(1, NYAW):
                one = jnp.where(of_yaw[yaw], picked[veer * NYAW + yaw], one)
            chosen = one if veer == 0 else jnp.where(veer_asked == float(veer), one, chosen)
        out_ref[group] = chosen


def rates(flag, spacing):
    column = lane_iota(1, LANES).astype(F32)
    rate = SIGMA_PEAK * 4.0 * (column + 1.0) * (FR - column) / float((FR + 1) ** 2)
    rate = jnp.where(column < FR, rate, 0.0) * flag
    column = lane_iota(CY, NX).astype(F32)
    row = row_iota(CY, NX)
    first_col = float(FR + NX // 16)
    away = column - first_col
    count = jnp.floor(away / spacing + 0.5)
    mask = (column >= first_col) & (column < NX - NX // 16) & (count * spacing == away)
    mask = mask & (row >= CY * 3 // 8) & (row < CY * 5 // 8)
    return rate, jnp.where(mask, flag, 0.0)


def change(u, stream, cross, west, east, north, south, above, below):
    total = (east + west) + (north + south) + (above + below) - 6.0 * u
    return 0.1 * (total - stream * (east - west) - cross * (north - south))


def begin_kernel(
    sample_ref, fields_ref, high_ref, low_ref, after_ref, before_ref, pred_ref, edge_ref, right_ref, const_ref
):
    flag = jnp.where(lax.axis_index("group") > 0, TIME_STEP, 0.0).astype(F32)
    spacing = ((sample_ref[0, 1] + 2) * (NX // 32)).astype(F32)
    rate, drag = rates(flag, spacing)
    yaw = sample_ref[0, 0]
    angles = np.float32(YAW_STEP) * (np.arange(NYAW, dtype=np.float32) - np.float32(1.5))
    cosine = jnp.float32(np.cos(angles[0]))
    sine = jnp.float32(np.sin(angles[0]))
    for at in range(1, NYAW):
        cosine = jnp.where(yaw == at, jnp.float32(np.cos(angles[at])), cosine)
        sine = jnp.where(yaw == at, jnp.float32(np.sin(angles[at])), sine)
    const_ref[0:CY, :] = drag[:, :LANES]
    const_ref[CY : CY + 1, :] = rate
    const_ref[CY + 1 : CY + 2, :] = jnp.full((1, LANES), cosine, F32)
    const_ref[CY + 2 : CY + 3, :] = jnp.full((1, LANES), sine, F32)
    const_ref[CY + 3 : CY + 8, :] = jnp.zeros((5, LANES), F32)
    rate = jnp.concatenate([rate, jnp.zeros((1, LANES), F32)], axis=1)
    row = row_iota(CY, NX)

    level_ids = row_iota(LEV, NX)
    for side in range(2):
        if side == 0:
            here = [before_ref[comp, 1] for comp in range(COMP)]
            south = [before_ref[comp, 0] for comp in range(COMP)]
            north = [low_ref[comp, 0] for comp in range(COMP)]
        else:
            here = [after_ref[comp, 0] for comp in range(COMP)]
            south = [high_ref[comp, 1] for comp in range(COMP)]
            north = [after_ref[comp, 1] for comp in range(COMP)]
        for comp in range(COMP):
            u = here[comp]
            below = jnp.where(level_ids == 0, -u, pltpu.roll(u, 1, 0))
            above = jnp.where(level_ids == LEV - 1, u, pltpu.roll(u, LEV - 1, 0))
            west, east = pltpu.roll(u, 1, 1), pltpu.roll(u, NX - 1, 1)
            moved = change(u, here[0], here[1], west, east, north[comp], south[comp], above, below)
            edge_ref[side, comp] = u + moved - rate * u

    for lev in range(LEV):
        stream, cross = fields_ref[0, 0, lev], fields_ref[0, 1, lev]
        loss = rate + drag * jnp.abs(stream) if 1 <= lev <= LEV // 2 else rate
        for comp in range(COMP):
            u = fields_ref[0, comp, lev]
            below = -u if lev == 0 else fields_ref[0, comp, lev - 1]
            above = u if lev == LEV - 1 else fields_ref[0, comp, lev + 1]
            north = jnp.where(row == CY - 1, after_ref[comp, 0, lev : lev + 1, :], pltpu.roll(u, CY - 1, 0))
            south = jnp.where(row == 0, before_ref[comp, 1, lev : lev + 1, :], pltpu.roll(u, 1, 0))
            west, east = pltpu.roll(u, 1, 1), pltpu.roll(u, NX - 1, 1)
            moved = change(u, stream, cross, west, east, north, south, above, below)
            pred_ref[comp, lev] = u + moved - loss * u

    row = row_iota(CY, LANES)
    lane = lane_iota(CY, LANES)
    for lev in range(LEV):
        stream, cross = pred_ref[0, lev, :, LANES:], pred_ref[1, lev, :, LANES:]
        for comp in range(COMP):
            u = pred_ref[comp, lev, :, LANES:]
            left = pred_ref[comp, lev, :, :LANES]
            below = -u if lev == 0 else pred_ref[comp, lev - 1, :, LANES:]
            above = u if lev == LEV - 1 else pred_ref[comp, lev + 1, :, LANES:]
            north = jnp.where(row == CY - 1, edge_ref[1, comp, lev : lev + 1, LANES:], pltpu.roll(u, CY - 1, 0))
            south = jnp.where(row == 0, edge_ref[0, comp, lev : lev + 1, LANES:], pltpu.roll(u, 1, 0))
            east = pltpu.roll(jnp.where(lane == 0, left, u), LANES - 1, 1)
            west = pltpu.roll(jnp.where(lane == LANES - 1, left, u), 1, 1)
            moved = change(u, stream, cross, west, east, north, south, above, below)
            if 1 <= lev <= LEV // 2:
                moved = moved - drag[:, LANES:] * jnp.abs(stream) * u
            right_ref[comp, lev] = 0.5 * (fields_ref[0, comp, lev, :, LANES:] + u + moved)


def finish_kernel(
    const_ref, fields_ref, planar_ref, pred_ref, edge_ref, right_ref, out_ref, unpacked, target, full, edge, result, sems
):
    drag = const_ref[0:CY, :]
    rate = const_ref[CY : CY + 1, :]
    cosine = const_ref[CY + 1 : CY + 2, :]
    sine = const_ref[CY + 2 : CY + 3, :]

    for lev in range(LEV):
        for half in range(2):
            packed = planar_ref[2 * lev + half]
            for part in range(4):
                turned = packed if part == 0 else pltpu.roll(packed, LANES - part * FR, 1)
                unpacked[2 * lev + half, 8 * part : 8 * part + 8, :] = turned
        aims = []
        for comp in range(COMP):
            parts = []
            for half in range(2):
                origin = comp if comp < 2 else half
                kind = 2 if comp == 2 else (half + comp) % 2
                parts.append(unpacked[2 * lev + origin, pl.ds(kind, HALF, stride=4), :])
            aims.append(jnp.concatenate(parts, axis=0))
        aims = [cosine * aims[0] - sine * aims[1], sine * aims[0] + cosine * aims[1], aims[2]]
        for comp in range(COMP):
            pull = rate * aims[comp]
            target[comp, lev] = pull
            full[comp, lev] = pred_ref[comp, lev, :, :LANES] + pull
    outer = [
        jnp.concatenate([planar_ref[2 * lev + at, 3:4, :] for lev in range(LEV)], axis=0) for at in range(2)
    ]
    for side in range(2):
        aims = []
        for comp in range(COMP):
            origin = comp if comp < 2 else side
            kind = 2 if comp == 2 else (side + comp) % 2
            packed = outer[origin]
            aims.append(packed if kind == 0 else pltpu.roll(packed, LANES - kind * FR, 1))
        aims = [cosine * aims[0] - sine * aims[1], sine * aims[0] + cosine * aims[1], aims[2]]
        for comp in range(COMP):
            edge[side, comp] = edge_ref[side, comp, :, :LANES] + rate * aims[comp]

    row = row_iota(CY, LANES)
    lane = lane_iota(CY, LANES)
    copies = []
    for lev in range(LEV):
        stream, cross = full[0, lev], full[1, lev]
        loss = rate + drag * jnp.abs(stream) if 1 <= lev <= LEV // 2 else rate
        last = 0.05 * (1.0 - pred_ref[0, lev, :, LANES:])
        for comp in range(COMP):
            u = full[comp, lev]
            right = pred_ref[comp, lev, :, LANES:]
            pull = target[comp, lev]
            below = -u if lev == 0 else full[comp, lev - 1]
            above = u if lev == LEV - 1 else full[comp, lev + 1]
            north = jnp.where(row == CY - 1, edge[1, comp, lev : lev + 1, :], pltpu.roll(u, CY - 1, 0))
            south = jnp.where(row == 0, edge[0, comp, lev : lev + 1, :], pltpu.roll(u, 1, 0))
            east = pltpu.roll(jnp.where(lane == 0, right, u), LANES - 1, 1)
            west = pltpu.roll(jnp.where(lane == LANES - 1, right, u), 1, 1)
            moved = change(u, stream, cross, west, east, north, south, above, below) + (pull - loss * u)
            result[comp, lev, :, :LANES] = 0.5 * (fields_ref[0, comp, lev, :, :LANES] + u + moved)
            passed = jnp.where(lane == LANES - 1, pltpu.roll(pull, LANES - 1, 1), 0.0)
            result[comp, lev, :, LANES:] = right_ref[comp, lev] + last * passed
        copy = pltpu.make_async_copy(result.at[:, lev], out_ref.at[0, :, lev], sems.at[lev])
        copy.start()
        copies.append(copy)
    for copy in copies:
        copy.wait()


def local(fields, sample_index, stencil, stencil_weight):
    message, low, high = pl.pallas_call(
        pack_kernel,
        out_shape=(shape(GROUPS, CY, LANES), shape(COMP, 2, LEV, NX), shape(COMP, 2, LEV, NX)),
        in_specs=[HBM, HBM],
        out_specs=(VMEM, VMEM, VMEM),
        scratch_shapes=[
            pltpu.SMEM((1, COMP), jnp.int32),
            pltpu.VMEM((2, COMP, LEV * CY, LANES), F32),
            pltpu.SemaphoreType.DMA((7,)),
        ],
        compiler_params=params(PACK_KIB),
        name="pack",
    )(sample_index, fields.reshape(COMP, LEV * CY, NX))
    up = [(i, (i + 1) % TILES) for i in range(TILES)]
    down = [(j, i) for i, j in up]
    after = lax.ppermute(low, "tile", down)
    before = lax.ppermute(high, "tile", up)
    asked = lax.all_to_all(message, "group", 0, 0, tiled=True)
    hot, spread = pl.pallas_call(
        prepare_kernel,
        out_shape=(
            shape(NY, 2 * CELLS * LANES, dtype=BF16),
            shape(2 * FR, 2 * CELLS * LANES),
        ),
        in_specs=[HBM, HBM],
        out_specs=(VMEM, VMEM),
        scratch_shapes=[
            pltpu.VMEM((2, NYAW, HALF, LANES), jnp.int32),
            pltpu.VMEM((2, NYAW, HALF, LANES), F32),
            pltpu.VMEM((2, NYAW, HALF, LANES), jnp.int32),
            pltpu.VMEM((2, NYAW, HALF, LANES), F32),
            pltpu.VMEM((512, 512), BF16),
            pltpu.SemaphoreType.DMA((2, 4)),
        ],
        compiler_params=params(),
        cost_estimate=cost(100_000_000_000, 200_000),
        name="prepare",
    )(stencil, stencil_weight)
    band = lax.all_to_all(
        jnp.broadcast_to(asked[0:1, :HALF], (TILES, HALF, LANES)),
        "tile",
        0,
        0,
        axis_index_groups=[TILE_ORDER],
        tiled=True,
    )
    pred, edge, right, const = pl.pallas_call(
        begin_kernel,
        out_shape=(
            shape(COMP, LEV, CY, NX),
            shape(2, COMP, LEV, NX),
            shape(COMP, LEV, CY, LANES),
            shape(CY + 8, LANES),
        ),
        in_specs=[SMEM] + [VMEM] * 5,
        out_specs=(VMEM, VMEM, VMEM, VMEM),
        compiler_params=params(),
        cost_estimate=cost(8_000_000, 1_000_000),
        name="begin",
    )(sample_index, fields, high, low, after, before)
    band, pred, edge, right, const = lax.optimization_barrier((band, pred, edge, right, const))
    answers = pl.pallas_call(
        interpolate_kernel,
        out_shape=shape(GROUPS, 8, LANES),
        in_specs=[VMEM] * 4,
        out_specs=VMEM,
        scratch_shapes=[
            pltpu.VMEM((NYAW * 8 * FR, NY), BF16),
            pltpu.VMEM((NYAW * NYAW, 8, LANES), F32),
            pltpu.VMEM((16, LANES), F32),
        ],
        compiler_params=params(),
        name="interpolate",
    )(band, asked, hot, spread)
    planar = lax.all_to_all(answers, "group", 0, 0, tiled=True)
    return pl.pallas_call(
        finish_kernel,
        out_shape=shape(1, COMP, LEV, CY, NX),
        in_specs=[VMEM] * 6,
        out_specs=HBM,
        scratch_shapes=[
            pltpu.VMEM((2 * LEV, 4 * HALF, LANES), F32),
            pltpu.VMEM((COMP, LEV, CY, LANES), F32),
            pltpu.VMEM((COMP, LEV, CY, LANES), F32),
            pltpu.VMEM((2, COMP, LEV, LANES), F32),
            pltpu.VMEM((COMP, LEV, CY, NX), F32),
            pltpu.SemaphoreType.DMA((LEV,)),
        ],
        compiler_params=params(),
        name="finish",
    )(const, fields, planar, pred, edge, right)


def solution(mesh):
    in_specs = (P("group", None, None, "tile", None), P("group", None), P(), P())
    out_specs = P("group", None, None, "tile", None)
    return jax.shard_map(local, mesh=mesh, in_specs=in_specs, out_specs=out_specs, check_vma=False)
```

```python
import jax
import jax.numpy as jnp
import numpy as np
from jax import lax
from jax.experimental import pallas as pl
from jax.experimental.pallas import tpu as pltpu
from jax.sharding import PartitionSpec as P

COMP = 3
LEV = 8
CY = 16
NX = 256
FR = 32
PACK_KIB = 60000
STEN = 4
NYAW = 4
GROUPS = 16
NY = 256
TILES = NY // CY
TILE_ORDER = [(tile + 11) % TILES for tile in range(TILES)]
GROUP_ORDER = [(group + 9) % GROUPS for group in range(GROUPS)]
HALF = CY // 2
LANES = 128
CELLS = 2 * NYAW + 1

TIME_STEP = 0.2
YAW_STEP = 0.2
SIGMA_PEAK = 2.5

F32 = jnp.float32
BF16 = jnp.bfloat16
VMEM = pl.BlockSpec(memory_space=pltpu.VMEM)
SMEM = pl.BlockSpec(memory_space=pltpu.SMEM)
HBM = pl.BlockSpec(memory_space=pltpu.HBM)


def params(kib=48 * 1024):
    return pltpu.CompilerParams(vmem_limit_bytes=kib * 1024)


def cost(flops, moved):
    return pl.CostEstimate(flops=flops, bytes_accessed=moved, transcendentals=0)


def shape(*dims, dtype=F32):
    return jax.ShapeDtypeStruct(dims, dtype)


def lane_iota(rows, lanes):
    return lax.broadcasted_iota(jnp.int32, (rows, lanes), 1)


def row_iota(rows, lanes):
    return lax.broadcasted_iota(jnp.int32, (rows, lanes), 0)


def pack_kernel(sample_hbm, fields_hbm, msg_ref, low_ref, high_ref, sample_ref, fields_ref, sems):
    sample_copy = pltpu.make_async_copy(sample_hbm, sample_ref, sems.at[0])
    sample_copy.start()
    halves = [pl.ds(NX - LANES, LANES), pl.ds(0, LANES)]
    copies = [
        [
            pltpu.make_async_copy(
                fields_hbm.at[comp, :, lanes], fields_ref.at[at, comp], sems.at[1 + 3 * at + comp]
            )
            for comp in range(COMP)
        ]
        for at, lanes in enumerate(halves)
    ]
    for part in copies:
        for copy in part:
            copy.start()
    for copy in copies[0]:
        copy.wait()
    sample_copy.wait()
    combo = (sample_ref[0, 2] * NYAW + sample_ref[0, 0]).astype(F32)
    lane = lane_iota(HALF, LANES)
    for lev in range(LEV):
        bands = [fields_ref[0, comp, lev * CY : (lev + 1) * CY, :] for comp in range(COMP)]
        for at in range(2):
            packed = pltpu.roll(bands[at][:HALF], FR, 1)
            packed = jnp.where(lane < FR, packed, pltpu.roll(bands[2][:HALF], 2 * FR, 1))
            packed = jnp.where(lane < 2 * FR, packed, pltpu.roll(bands[at][HALF:], 3 * FR, 1))
            packed = jnp.where(lane < 3 * FR, packed, bands[2][HALF:])
            msg_ref[2 * lev + at, 0:HALF, :] = packed
            msg_ref[2 * lev + at, HALF:CY, :] = jnp.full((HALF, LANES), combo, F32)
    for copy in copies[1]:
        copy.wait()
    for comp in range(COMP):
        for row in range(2):
            for at, lanes in enumerate(halves):
                part = fields_ref.at[at, comp]
                low_ref[comp, row, :, lanes] = part[pl.ds(row, LEV, stride=CY), :]
                high_ref[comp, row, :, lanes] = part[pl.ds(CY - 2 + row, LEV, stride=CY), :]


def prepare_kernel(
    stencil_ref, weight_ref, hot_ref, spread_ref, sten, wts, sten_x, wts_x, perm, sems
):
    halves = [lax.axis_index("group") % 2, 1 - lax.axis_index("group") % 2]
    copies = []
    for slot, half in enumerate(halves):
        start = lax.axis_index("tile") * CY + half * HALF
        beyond = (start + jnp.where(half == 0, NY - HALF, HALF)) % NY
        start = pl.multiple_of(start, HALF)
        beyond = pl.multiple_of(beyond, HALF)
        copies += [
            pltpu.make_async_copy(stencil_ref.at[:, pl.ds(start, HALF), :], sten.at[slot], sems.at[slot, 0]),
            pltpu.make_async_copy(weight_ref.at[:, pl.ds(start, HALF), :], wts.at[slot], sems.at[slot, 1]),
            pltpu.make_async_copy(stencil_ref.at[:, pl.ds(beyond, HALF), :], sten_x.at[slot], sems.at[slot, 2]),
            pltpu.make_async_copy(weight_ref.at[:, pl.ds(beyond, HALF), :], wts_x.at[slot], sems.at[slot, 3]),
        ]
    for copy in copies:
        copy.start()
    source = row_iota(512, 512)
    target = (source % 4) * LANES + (source // LANES) * FR + (source % LANES) // 4
    perm[...] = jnp.where(target == lane_iota(512, 512), 1.0, 0.0).astype(BF16)
    for copy in copies:
        copy.wait()

    def gathered(main, extra):
        parts = []
        for part in range(4):
            rows = []
            for slot, half in enumerate(halves):
                rows += [main[slot, yaw, 2 * part : 2 * part + 2, :] for yaw in range(NYAW)]
                outer = jnp.where(
                    half == 0, extra[slot, part, HALF - 1 : HALF, :], extra[slot, part, 0:1, :]
                )
                rows.append(outer)
                rows.append(jnp.zeros((7, LANES), outer.dtype))
            parts.append(jnp.concatenate(rows, axis=0))
        return jnp.concatenate(parts, axis=1)

    index = gathered(sten, sten_x)
    weight = gathered(wts, wts_x)
    first = weight.astype(BF16)
    rest = weight - first.astype(F32)
    second = rest.astype(BF16)
    third = (rest - second.astype(F32)).astype(BF16)
    source_row = (index >> 5).astype(F32).astype(BF16)
    source_col = (index & 31).astype(F32).astype(BF16)
    stacked = jnp.concatenate([source_row, source_col, first, second, third], axis=0)
    sorted_ = jnp.dot(stacked, perm[...], preferred_element_type=F32)
    weight = (sorted_[64:96] + sorted_[96:128]) + sorted_[128:160]
    rows = [sorted_[0:32, k * LANES : (k + 1) * LANES] for k in range(STEN)]
    cols = [sorted_[32:64, k * LANES : (k + 1) * LANES] for k in range(STEN)]
    below = jnp.zeros((32, LANES), F32)
    for k in range(1, STEN):
        delta = rows[k] - rows[0]
        below = jnp.where((delta == -1.0) | (delta == NY - 1.0), 1.0, below)
    base = rows[0] - below
    base = jnp.where(base < 0.0, base + NY, base)
    keys = []
    for k in range(STEN):
        offset = rows[k] - base
        offset = jnp.where(offset < 0.0, offset + NY, offset)
        keys.append(offset * FR + cols[k])
    row_ids = row_iota(NY, LANES).astype(F32)
    key_ids = row_iota(2 * FR, LANES).astype(F32)
    for cell in range(2 * CELLS):
        at = 16 * (cell // CELLS) + cell % CELLS
        lanes = slice(cell * LANES, (cell + 1) * LANES)
        hot_ref[:, lanes] = jnp.where(row_ids == base[at : at + 1], 1.0, 0.0).astype(BF16)
        spread = jnp.zeros((2 * FR, LANES), F32)
        for k in range(STEN):
            share = weight[at : at + 1, k * LANES : (k + 1) * LANES]
            spread = spread + jnp.where(key_ids == keys[k][at : at + 1], share, 0.0)
        spread_ref[:, lanes] = spread


def interpolate_kernel(
    band_ref, asked_ref, hot_ref, spread_ref, out_ref, table, picked, outer
):
    level = lax.axis_index("group") // 2
    blocks = []
    for tile in range(TILES):
        block = band_ref[TILE_ORDER.index(tile)]
        blocks += [block, pltpu.roll(block, 2 * FR, 1)]
    band = jnp.concatenate(blocks, axis=0).T[: 2 * FR]
    rows = NYAW * 2 * FR
    for veer in range(NYAW):
        for step in range(2):
            shift = (NY - (veer * (level + 1) * (CY // 4) + step)) % NY
            moved = band if veer + step == 0 else pltpu.roll(band, shift, 1)
            upper = moved.astype(BF16)
            lower = (moved - upper.astype(F32)).astype(BF16)
            for plane in range(2):
                at = 2 * plane * rows + (veer * 2 + step) * FR
                table[at : at + FR, :] = upper[plane * FR : (plane + 1) * FR]
                table[at + rows : at + rows + FR, :] = lower[plane * FR : (plane + 1) * FR]
    for slot in range(2):
        planes = 2 - slot
        for pair in range(5):
            cells = [cell for cell in (2 * pair, 2 * pair + 1) if cell < CELLS]
            first = slot * CELLS + 2 * pair
            ones = hot_ref[:, first * LANES : (first + len(cells)) * LANES]
            product = jnp.dot(table[0 : 2 * planes * rows], ones, preferred_element_type=F32)
            for at, cell in enumerate(cells):
                weights = spread_ref[:, (first + at) * LANES : (first + at + 1) * LANES]
                for plane in range(planes):
                    kind = 2 if plane == 1 else slot
                    for veer in range(NYAW):
                        top = 2 * plane * rows + veer * 2 * FR
                        span = slice(at * LANES, (at + 1) * LANES)
                        upper = product[top : top + 2 * FR, span]
                        lower = product[top + rows : top + rows + 2 * FR, span]
                        value = jnp.sum((upper + lower) * weights, axis=0, keepdims=True)
                        if cell < 2 * NYAW:
                            yaw, j = divmod(cell, 2)
                            picked[veer * NYAW + yaw, 4 * j + kind : 4 * j + kind + 1, :] = value
                        else:
                            outer[veer * COMP + kind : veer * COMP + kind + 1, :] = value
    lane = lane_iota(1, LANES)
    rolled = [outer[...] if turn == 0 else pltpu.roll(outer[...], turn * FR, 1) for turn in range(4)]
    for veer in range(NYAW):
        for yaw in range(NYAW):
            rows = [
                rolled[(comp - yaw) % 4][veer * COMP + comp : veer * COMP + comp + 1] for comp in range(COMP)
            ]
            row = jnp.where(lane < FR, rows[0], jnp.where(lane < 2 * FR, rows[1], rows[2]))
            picked[veer * NYAW + yaw, 3:4, :] = row
            picked[veer * NYAW + yaw, 7:8, :] = row
    for group in range(GROUPS):
        asked = asked_ref[group, HALF:CY, :]
        veer_asked = jnp.floor(asked * (1.0 / NYAW))
        yaw_asked = asked - NYAW * veer_asked
        of_yaw = [yaw_asked == float(yaw) for yaw in range(NYAW)]
        chosen = None
        for veer in range(NYAW):
            one = picked[veer * NYAW]
            for yaw in range(1, NYAW):
                one = jnp.where(of_yaw[yaw], picked[veer * NYAW + yaw], one)
            chosen = one if veer == 0 else jnp.where(veer_asked == float(veer), one, chosen)
        out_ref[GROUP_ORDER.index(group)] = chosen


def rates(flag, spacing):
    column = lane_iota(1, LANES).astype(F32)
    rate = SIGMA_PEAK * 4.0 * (column + 1.0) * (FR - column) / float((FR + 1) ** 2)
    rate = jnp.where(column < FR, rate, 0.0) * flag
    column = lane_iota(CY, NX).astype(F32)
    row = row_iota(CY, NX)
    first_col = float(FR + NX // 16)
    away = column - first_col
    count = jnp.floor(away / spacing + 0.5)
    mask = (column >= first_col) & (column < NX - NX // 16) & (count * spacing == away)
    mask = mask & (row >= CY * 3 // 8) & (row < CY * 5 // 8)
    return rate, jnp.where(mask, flag, 0.0)


def change(u, stream, cross, west, east, north, south, above, below):
    total = (east + west) + (north + south) + (above + below) - 6.0 * u
    return 0.1 * (total - stream * (east - west) - cross * (north - south))


def begin_kernel(
    sample_ref, fields_ref, high_ref, low_ref, after_ref, before_ref, pred_ref, edge_ref, right_ref, const_ref
):
    flag = jnp.where(lax.axis_index("group") > 0, TIME_STEP, 0.0).astype(F32)
    spacing = ((sample_ref[0, 1] + 2) * (NX // 32)).astype(F32)
    rate, drag = rates(flag, spacing)
    yaw = sample_ref[0, 0]
    angles = np.float32(YAW_STEP) * (np.arange(NYAW, dtype=np.float32) - np.float32(1.5))
    cosine = jnp.float32(np.cos(angles[0]))
    sine = jnp.float32(np.sin(angles[0]))
    for at in range(1, NYAW):
        cosine = jnp.where(yaw == at, jnp.float32(np.cos(angles[at])), cosine)
        sine = jnp.where(yaw == at, jnp.float32(np.sin(angles[at])), sine)
    const_ref[0:CY, :] = drag[:, :LANES]
    const_ref[CY : CY + 1, :] = rate
    const_ref[CY + 1 : CY + 2, :] = jnp.full((1, LANES), cosine, F32)
    const_ref[CY + 2 : CY + 3, :] = jnp.full((1, LANES), sine, F32)
    const_ref[CY + 3 : CY + 8, :] = jnp.zeros((5, LANES), F32)
    rate = jnp.concatenate([rate, jnp.zeros((1, LANES), F32)], axis=1)
    row = row_iota(CY, NX)

    level_ids = row_iota(LEV, NX)
    for side in range(2):
        if side == 0:
            here = [before_ref[comp, 1] for comp in range(COMP)]
            south = [before_ref[comp, 0] for comp in range(COMP)]
            north = [low_ref[comp, 0] for comp in range(COMP)]
        else:
            here = [after_ref[comp, 0] for comp in range(COMP)]
            south = [high_ref[comp, 1] for comp in range(COMP)]
            north = [after_ref[comp, 1] for comp in range(COMP)]
        for comp in range(COMP):
            u = here[comp]
            below = jnp.where(level_ids == 0, -u, pltpu.roll(u, 1, 0))
            above = jnp.where(level_ids == LEV - 1, u, pltpu.roll(u, LEV - 1, 0))
            west, east = pltpu.roll(u, 1, 1), pltpu.roll(u, NX - 1, 1)
            moved = change(u, here[0], here[1], west, east, north[comp], south[comp], above, below)
            edge_ref[side, comp] = u + moved - rate * u

    for lev in range(LEV):
        stream, cross = fields_ref[0, 0, lev], fields_ref[0, 1, lev]
        loss = rate + drag * jnp.abs(stream) if 1 <= lev <= LEV // 2 else rate
        for comp in range(COMP):
            u = fields_ref[0, comp, lev]
            below = -u if lev == 0 else fields_ref[0, comp, lev - 1]
            above = u if lev == LEV - 1 else fields_ref[0, comp, lev + 1]
            north = jnp.where(row == CY - 1, after_ref[comp, 0, lev : lev + 1, :], pltpu.roll(u, CY - 1, 0))
            south = jnp.where(row == 0, before_ref[comp, 1, lev : lev + 1, :], pltpu.roll(u, 1, 0))
            west, east = pltpu.roll(u, 1, 1), pltpu.roll(u, NX - 1, 1)
            moved = change(u, stream, cross, west, east, north, south, above, below)
            pred_ref[comp, lev] = u + moved - loss * u

    row = row_iota(CY, LANES)
    lane = lane_iota(CY, LANES)
    for lev in range(LEV):
        stream, cross = pred_ref[0, lev, :, LANES:], pred_ref[1, lev, :, LANES:]
        for comp in range(COMP):
            u = pred_ref[comp, lev, :, LANES:]
            left = pred_ref[comp, lev, :, :LANES]
            below = -u if lev == 0 else pred_ref[comp, lev - 1, :, LANES:]
            above = u if lev == LEV - 1 else pred_ref[comp, lev + 1, :, LANES:]
            north = jnp.where(row == CY - 1, edge_ref[1, comp, lev : lev + 1, LANES:], pltpu.roll(u, CY - 1, 0))
            south = jnp.where(row == 0, edge_ref[0, comp, lev : lev + 1, LANES:], pltpu.roll(u, 1, 0))
            east = pltpu.roll(jnp.where(lane == 0, left, u), LANES - 1, 1)
            west = pltpu.roll(jnp.where(lane == LANES - 1, left, u), 1, 1)
            moved = change(u, stream, cross, west, east, north, south, above, below)
            if 1 <= lev <= LEV // 2:
                moved = moved - drag[:, LANES:] * jnp.abs(stream) * u
            right_ref[comp, lev] = 0.5 * (fields_ref[0, comp, lev, :, LANES:] + u + moved)


def finish_kernel(
    const_ref, fields_ref, planar_ref, pred_ref, edge_ref, right_ref, out_ref, unpacked, target, full, edge, result, sems
):
    drag = const_ref[0:CY, :]
    rate = const_ref[CY : CY + 1, :]
    cosine = const_ref[CY + 1 : CY + 2, :]
    sine = const_ref[CY + 2 : CY + 3, :]

    for lev in range(LEV):
        for half in range(2):
            packed = planar_ref[GROUP_ORDER.index(2 * lev + half)]
            for part in range(4):
                turned = packed if part == 0 else pltpu.roll(packed, LANES - part * FR, 1)
                unpacked[2 * lev + half, 8 * part : 8 * part + 8, :] = turned
        aims = []
        for comp in range(COMP):
            parts = []
            for half in range(2):
                origin = comp if comp < 2 else half
                kind = 2 if comp == 2 else (half + comp) % 2
                parts.append(unpacked[2 * lev + origin, pl.ds(kind, HALF, stride=4), :])
            aims.append(jnp.concatenate(parts, axis=0))
        aims = [cosine * aims[0] - sine * aims[1], sine * aims[0] + cosine * aims[1], aims[2]]
        for comp in range(COMP):
            pull = rate * aims[comp]
            target[comp, lev] = pull
            full[comp, lev] = pred_ref[comp, lev, :, :LANES] + pull
    outer = [
        jnp.concatenate([planar_ref[GROUP_ORDER.index(2 * lev + at), 3:4, :] for lev in range(LEV)], axis=0) for at in range(2)
    ]
    for side in range(2):
        aims = []
        for comp in range(COMP):
            origin = comp if comp < 2 else side
            kind = 2 if comp == 2 else (side + comp) % 2
            packed = outer[origin]
            aims.append(packed if kind == 0 else pltpu.roll(packed, LANES - kind * FR, 1))
        aims = [cosine * aims[0] - sine * aims[1], sine * aims[0] + cosine * aims[1], aims[2]]
        for comp in range(COMP):
            edge[side, comp] = edge_ref[side, comp, :, :LANES] + rate * aims[comp]

    row = row_iota(CY, LANES)
    lane = lane_iota(CY, LANES)
    copies = []
    for lev in range(LEV):
        stream, cross = full[0, lev], full[1, lev]
        loss = rate + drag * jnp.abs(stream) if 1 <= lev <= LEV // 2 else rate
        last = 0.05 * (1.0 - pred_ref[0, lev, :, LANES:])
        for comp in range(COMP):
            u = full[comp, lev]
            right = pred_ref[comp, lev, :, LANES:]
            pull = target[comp, lev]
            below = -u if lev == 0 else full[comp, lev - 1]
            above = u if lev == LEV - 1 else full[comp, lev + 1]
            north = jnp.where(row == CY - 1, edge[1, comp, lev : lev + 1, :], pltpu.roll(u, CY - 1, 0))
            south = jnp.where(row == 0, edge[0, comp, lev : lev + 1, :], pltpu.roll(u, 1, 0))
            east = pltpu.roll(jnp.where(lane == 0, right, u), LANES - 1, 1)
            west = pltpu.roll(jnp.where(lane == LANES - 1, right, u), 1, 1)
            moved = change(u, stream, cross, west, east, north, south, above, below) + (pull - loss * u)
            result[comp, lev, :, :LANES] = 0.5 * (fields_ref[0, comp, lev, :, :LANES] + u + moved)
            passed = jnp.where(lane == LANES - 1, pltpu.roll(pull, LANES - 1, 1), 0.0)
            result[comp, lev, :, LANES:] = right_ref[comp, lev] + last * passed
        copy = pltpu.make_async_copy(result.at[:, lev], out_ref.at[0, :, lev], sems.at[lev])
        copy.start()
        copies.append(copy)
    for copy in copies:
        copy.wait()


def local(fields, sample_index, stencil, stencil_weight):
    message, low, high = pl.pallas_call(
        pack_kernel,
        out_shape=(shape(GROUPS, CY, LANES), shape(COMP, 2, LEV, NX), shape(COMP, 2, LEV, NX)),
        in_specs=[HBM, HBM],
        out_specs=(VMEM, VMEM, VMEM),
        scratch_shapes=[
            pltpu.SMEM((1, COMP), jnp.int32),
            pltpu.VMEM((2, COMP, LEV * CY, LANES), F32),
            pltpu.SemaphoreType.DMA((7,)),
        ],
        compiler_params=params(PACK_KIB),
        name="pack",
    )(sample_index, fields.reshape(COMP, LEV * CY, NX))
    up = [(i, (i + 1) % TILES) for i in range(TILES)]
    down = [(j, i) for i, j in up]
    after = lax.ppermute(low, "tile", down)
    before = lax.ppermute(high, "tile", up)
    asked = lax.all_to_all(message, "group", 0, 0, tiled=True)
    hot, spread = pl.pallas_call(
        prepare_kernel,
        out_shape=(
            shape(NY, 2 * CELLS * LANES, dtype=BF16),
            shape(2 * FR, 2 * CELLS * LANES),
        ),
        in_specs=[HBM, HBM],
        out_specs=(VMEM, VMEM),
        scratch_shapes=[
            pltpu.VMEM((2, NYAW, HALF, LANES), jnp.int32),
            pltpu.VMEM((2, NYAW, HALF, LANES), F32),
            pltpu.VMEM((2, NYAW, HALF, LANES), jnp.int32),
            pltpu.VMEM((2, NYAW, HALF, LANES), F32),
            pltpu.VMEM((512, 512), BF16),
            pltpu.SemaphoreType.DMA((2, 4)),
        ],
        compiler_params=params(),
        cost_estimate=cost(100_000_000_000, 200_000),
        name="prepare",
    )(stencil, stencil_weight)
    band = lax.all_to_all(
        jnp.broadcast_to(asked[0:1, :HALF], (TILES, HALF, LANES)),
        "tile",
        0,
        0,
        axis_index_groups=[TILE_ORDER],
        tiled=True,
    )
    pred, edge, right, const = pl.pallas_call(
        begin_kernel,
        out_shape=(
            shape(COMP, LEV, CY, NX),
            shape(2, COMP, LEV, NX),
            shape(COMP, LEV, CY, LANES),
            shape(CY + 8, LANES),
        ),
        in_specs=[SMEM] + [VMEM] * 5,
        out_specs=(VMEM, VMEM, VMEM, VMEM),
        compiler_params=params(),
        cost_estimate=cost(8_000_000, 1_000_000),
        name="begin",
    )(sample_index, fields, high, low, after, before)
    band, pred, edge, right, const = lax.optimization_barrier((band, pred, edge, right, const))
    answers = pl.pallas_call(
        interpolate_kernel,
        out_shape=shape(GROUPS, 8, LANES),
        in_specs=[VMEM] * 4,
        out_specs=VMEM,
        scratch_shapes=[
            pltpu.VMEM((NYAW * 8 * FR, NY), BF16),
            pltpu.VMEM((NYAW * NYAW, 8, LANES), F32),
            pltpu.VMEM((16, LANES), F32),
        ],
        compiler_params=params(),
        name="interpolate",
    )(band, asked, hot, spread)
    planar = lax.all_to_all(answers, "group", 0, 0, axis_index_groups=[GROUP_ORDER], tiled=True)
    return pl.pallas_call(
        finish_kernel,
        out_shape=shape(1, COMP, LEV, CY, NX),
        in_specs=[VMEM] * 6,
        out_specs=HBM,
        scratch_shapes=[
            pltpu.VMEM((2 * LEV, 4 * HALF, LANES), F32),
            pltpu.VMEM((COMP, LEV, CY, LANES), F32),
            pltpu.VMEM((COMP, LEV, CY, LANES), F32),
            pltpu.VMEM((2, COMP, LEV, LANES), F32),
            pltpu.VMEM((COMP, LEV, CY, NX), F32),
            pltpu.SemaphoreType.DMA((LEV,)),
        ],
        compiler_params=params(),
        name="finish",
    )(const, fields, planar, pred, edge, right)


def solution(mesh):
    in_specs = (P("group", None, None, "tile", None), P("group", None), P(), P())
    out_specs = P("group", None, None, "tile", None)
    return jax.shard_map(local, mesh=mesh, in_specs=in_specs, out_specs=out_specs, check_vma=False)
```

```python
import jax
import jax.numpy as jnp
import numpy as np
from jax import lax
from jax.experimental import pallas as pl
from jax.experimental.pallas import tpu as pltpu
from jax.sharding import PartitionSpec as P

COMP = 3
LEV = 8
CY = 16
NX = 256
FR = 32
PACK_KIB = 60000
STEN = 4
NYAW = 4
GROUPS = 16
NY = 256
TILES = NY // CY
TILE_ORDER = [(tile + 11) % TILES for tile in range(TILES)]
GROUP_ORDER = [(group + 13) % GROUPS for group in range(GROUPS)]
HALF = CY // 2
LANES = 128
CELLS = 2 * NYAW + 1

TIME_STEP = 0.2
YAW_STEP = 0.2
SIGMA_PEAK = 2.5

F32 = jnp.float32
BF16 = jnp.bfloat16
VMEM = pl.BlockSpec(memory_space=pltpu.VMEM)
SMEM = pl.BlockSpec(memory_space=pltpu.SMEM)
HBM = pl.BlockSpec(memory_space=pltpu.HBM)


def params(kib=48 * 1024):
    return pltpu.CompilerParams(vmem_limit_bytes=kib * 1024)


def cost(flops, moved):
    return pl.CostEstimate(flops=flops, bytes_accessed=moved, transcendentals=0)


def shape(*dims, dtype=F32):
    return jax.ShapeDtypeStruct(dims, dtype)


def lane_iota(rows, lanes):
    return lax.broadcasted_iota(jnp.int32, (rows, lanes), 1)


def row_iota(rows, lanes):
    return lax.broadcasted_iota(jnp.int32, (rows, lanes), 0)


def pack_kernel(sample_hbm, fields_hbm, msg_ref, low_ref, high_ref, sample_ref, fields_ref, sems):
    sample_copy = pltpu.make_async_copy(sample_hbm, sample_ref, sems.at[0])
    sample_copy.start()
    halves = [pl.ds(NX - LANES, LANES), pl.ds(0, LANES)]
    copies = [
        [
            pltpu.make_async_copy(
                fields_hbm.at[comp, :, lanes], fields_ref.at[at, comp], sems.at[1 + 3 * at + comp]
            )
            for comp in range(COMP)
        ]
        for at, lanes in enumerate(halves)
    ]
    for part in copies:
        for copy in part:
            copy.start()
    for copy in copies[0]:
        copy.wait()
    sample_copy.wait()
    combo = (sample_ref[0, 2] * NYAW + sample_ref[0, 0]).astype(F32)
    lane = lane_iota(HALF, LANES)
    for lev in range(LEV):
        bands = [fields_ref[0, comp, lev * CY : (lev + 1) * CY, :] for comp in range(COMP)]
        for at in range(2):
            packed = pltpu.roll(bands[at][:HALF], FR, 1)
            packed = jnp.where(lane < FR, packed, pltpu.roll(bands[2][:HALF], 2 * FR, 1))
            packed = jnp.where(lane < 2 * FR, packed, pltpu.roll(bands[at][HALF:], 3 * FR, 1))
            packed = jnp.where(lane < 3 * FR, packed, bands[2][HALF:])
            msg_ref[2 * lev + at, 0:HALF, :] = packed
            msg_ref[2 * lev + at, HALF:CY, :] = jnp.full((HALF, LANES), combo, F32)
    for copy in copies[1]:
        copy.wait()
    for comp in range(COMP):
        for row in range(2):
            for at, lanes in enumerate(halves):
                part = fields_ref.at[at, comp]
                low_ref[comp, row, :, lanes] = part[pl.ds(row, LEV, stride=CY), :]
                high_ref[comp, row, :, lanes] = part[pl.ds(CY - 2 + row, LEV, stride=CY), :]


def prepare_kernel(
    stencil_ref, weight_ref, hot_ref, spread_ref, sten, wts, sten_x, wts_x, perm, sems
):
    halves = [lax.axis_index("group") % 2, 1 - lax.axis_index("group") % 2]
    copies = []
    for slot, half in enumerate(halves):
        start = lax.axis_index("tile") * CY + half * HALF
        beyond = (start + jnp.where(half == 0, NY - HALF, HALF)) % NY
        start = pl.multiple_of(start, HALF)
        beyond = pl.multiple_of(beyond, HALF)
        copies += [
            pltpu.make_async_copy(stencil_ref.at[:, pl.ds(start, HALF), :], sten.at[slot], sems.at[slot, 0]),
            pltpu.make_async_copy(weight_ref.at[:, pl.ds(start, HALF), :], wts.at[slot], sems.at[slot, 1]),
            pltpu.make_async_copy(stencil_ref.at[:, pl.ds(beyond, HALF), :], sten_x.at[slot], sems.at[slot, 2]),
            pltpu.make_async_copy(weight_ref.at[:, pl.ds(beyond, HALF), :], wts_x.at[slot], sems.at[slot, 3]),
        ]
    for copy in copies:
        copy.start()
    source = row_iota(512, 512)
    target = (source % 4) * LANES + (source // LANES) * FR + (source % LANES) // 4
    perm[...] = jnp.where(target == lane_iota(512, 512), 1.0, 0.0).astype(BF16)
    for copy in copies:
        copy.wait()

    def gathered(main, extra):
        parts = []
        for part in range(4):
            rows = []
            for slot, half in enumerate(halves):
                rows += [main[slot, yaw, 2 * part : 2 * part + 2, :] for yaw in range(NYAW)]
                outer = jnp.where(
                    half == 0, extra[slot, part, HALF - 1 : HALF, :], extra[slot, part, 0:1, :]
                )
                rows.append(outer)
                rows.append(jnp.zeros((7, LANES), outer.dtype))
            parts.append(jnp.concatenate(rows, axis=0))
        return jnp.concatenate(parts, axis=1)

    index = gathered(sten, sten_x)
    weight = gathered(wts, wts_x)
    first = weight.astype(BF16)
    rest = weight - first.astype(F32)
    second = rest.astype(BF16)
    third = (rest - second.astype(F32)).astype(BF16)
    source_row = (index >> 5).astype(F32).astype(BF16)
    source_col = (index & 31).astype(F32).astype(BF16)
    stacked = jnp.concatenate([source_row, source_col, first, second, third], axis=0)
    sorted_ = jnp.dot(stacked, perm[...], preferred_element_type=F32)
    weight = (sorted_[64:96] + sorted_[96:128]) + sorted_[128:160]
    rows = [sorted_[0:32, k * LANES : (k + 1) * LANES] for k in range(STEN)]
    cols = [sorted_[32:64, k * LANES : (k + 1) * LANES] for k in range(STEN)]
    below = jnp.zeros((32, LANES), F32)
    for k in range(1, STEN):
        delta = rows[k] - rows[0]
        below = jnp.where((delta == -1.0) | (delta == NY - 1.0), 1.0, below)
    base = rows[0] - below
    base = jnp.where(base < 0.0, base + NY, base)
    keys = []
    for k in range(STEN):
        offset = rows[k] - base
        offset = jnp.where(offset < 0.0, offset + NY, offset)
        keys.append(offset * FR + cols[k])
    row_ids = row_iota(NY, LANES).astype(F32)
    key_ids = row_iota(2 * FR, LANES).astype(F32)
    for cell in range(2 * CELLS):
        at = 16 * (cell // CELLS) + cell % CELLS
        lanes = slice(cell * LANES, (cell + 1) * LANES)
        hot_ref[:, lanes] = jnp.where(row_ids == base[at : at + 1], 1.0, 0.0).astype(BF16)
        spread = jnp.zeros((2 * FR, LANES), F32)
        for k in range(STEN):
            share = weight[at : at + 1, k * LANES : (k + 1) * LANES]
            spread = spread + jnp.where(key_ids == keys[k][at : at + 1], share, 0.0)
        spread_ref[:, lanes] = spread


def interpolate_kernel(
    band_ref, asked_ref, hot_ref, spread_ref, out_ref, table, picked, outer
):
    level = lax.axis_index("group") // 2
    blocks = []
    for tile in range(TILES):
        block = band_ref[TILE_ORDER.index(tile)]
        blocks += [block, pltpu.roll(block, 2 * FR, 1)]
    band = jnp.concatenate(blocks, axis=0).T[: 2 * FR]
    rows = NYAW * 2 * FR
    for veer in range(NYAW):
        for step in range(2):
            shift = (NY - (veer * (level + 1) * (CY // 4) + step)) % NY
            moved = band if veer + step == 0 else pltpu.roll(band, shift, 1)
            upper = moved.astype(BF16)
            lower = (moved - upper.astype(F32)).astype(BF16)
            for plane in range(2):
                at = 2 * plane * rows + (veer * 2 + step) * FR
                table[at : at + FR, :] = upper[plane * FR : (plane + 1) * FR]
                table[at + rows : at + rows + FR, :] = lower[plane * FR : (plane + 1) * FR]
    for slot in range(2):
        planes = 2 - slot
        for pair in range(5):
            cells = [cell for cell in (2 * pair, 2 * pair + 1) if cell < CELLS]
            first = slot * CELLS + 2 * pair
            ones = hot_ref[:, first * LANES : (first + len(cells)) * LANES]
            product = jnp.dot(table[0 : 2 * planes * rows], ones, preferred_element_type=F32)
            for at, cell in enumerate(cells):
                weights = spread_ref[:, (first + at) * LANES : (first + at + 1) * LANES]
                for plane in range(planes):
                    kind = 2 if plane == 1 else slot
                    for veer in range(NYAW):
                        top = 2 * plane * rows + veer * 2 * FR
                        span = slice(at * LANES, (at + 1) * LANES)
                        upper = product[top : top + 2 * FR, span]
                        lower = product[top + rows : top + rows + 2 * FR, span]
                        value = jnp.sum((upper + lower) * weights, axis=0, keepdims=True)
                        if cell < 2 * NYAW:
                            yaw, j = divmod(cell, 2)
                            picked[veer * NYAW + yaw, 4 * j + kind : 4 * j + kind + 1, :] = value
                        else:
                            outer[veer * COMP + kind : veer * COMP + kind + 1, :] = value
    lane = lane_iota(1, LANES)
    rolled = [outer[...] if turn == 0 else pltpu.roll(outer[...], turn * FR, 1) for turn in range(4)]
    for veer in range(NYAW):
        for yaw in range(NYAW):
            rows = [
                rolled[(comp - yaw) % 4][veer * COMP + comp : veer * COMP + comp + 1] for comp in range(COMP)
            ]
            row = jnp.where(lane < FR, rows[0], jnp.where(lane < 2 * FR, rows[1], rows[2]))
            picked[veer * NYAW + yaw, 3:4, :] = row
            picked[veer * NYAW + yaw, 7:8, :] = row
    for group in range(GROUPS):
        asked = asked_ref[group, HALF:CY, :]
        veer_asked = jnp.floor(asked * (1.0 / NYAW))
        yaw_asked = asked - NYAW * veer_asked
        of_yaw = [yaw_asked == float(yaw) for yaw in range(NYAW)]
        chosen = None
        for veer in range(NYAW):
            one = picked[veer * NYAW]
            for yaw in range(1, NYAW):
                one = jnp.where(of_yaw[yaw], picked[veer * NYAW + yaw], one)
            chosen = one if veer == 0 else jnp.where(veer_asked == float(veer), one, chosen)
        out_ref[GROUP_ORDER.index(group)] = chosen


def rates(flag, spacing):
    column = lane_iota(1, LANES).astype(F32)
    rate = SIGMA_PEAK * 4.0 * (column + 1.0) * (FR - column) / float((FR + 1) ** 2)
    rate = jnp.where(column < FR, rate, 0.0) * flag
    column = lane_iota(CY, NX).astype(F32)
    row = row_iota(CY, NX)
    first_col = float(FR + NX // 16)
    away = column - first_col
    count = jnp.floor(away / spacing + 0.5)
    mask = (column >= first_col) & (column < NX - NX // 16) & (count * spacing == away)
    mask = mask & (row >= CY * 3 // 8) & (row < CY * 5 // 8)
    return rate, jnp.where(mask, flag, 0.0)


def change(u, stream, cross, west, east, north, south, above, below):
    total = (east + west) + (north + south) + (above + below) - 6.0 * u
    return 0.1 * (total - stream * (east - west) - cross * (north - south))


def begin_kernel(
    sample_ref, fields_ref, high_ref, low_ref, after_ref, before_ref, pred_ref, edge_ref, right_ref, const_ref
):
    flag = jnp.where(lax.axis_index("group") > 0, TIME_STEP, 0.0).astype(F32)
    spacing = ((sample_ref[0, 1] + 2) * (NX // 32)).astype(F32)
    rate, drag = rates(flag, spacing)
    yaw = sample_ref[0, 0]
    angles = np.float32(YAW_STEP) * (np.arange(NYAW, dtype=np.float32) - np.float32(1.5))
    cosine = jnp.float32(np.cos(angles[0]))
    sine = jnp.float32(np.sin(angles[0]))
    for at in range(1, NYAW):
        cosine = jnp.where(yaw == at, jnp.float32(np.cos(angles[at])), cosine)
        sine = jnp.where(yaw == at, jnp.float32(np.sin(angles[at])), sine)
    const_ref[0:CY, :] = drag[:, :LANES]
    const_ref[CY : CY + 1, :] = rate
    const_ref[CY + 1 : CY + 2, :] = jnp.full((1, LANES), cosine, F32)
    const_ref[CY + 2 : CY + 3, :] = jnp.full((1, LANES), sine, F32)
    const_ref[CY + 3 : CY + 8, :] = jnp.zeros((5, LANES), F32)
    rate = jnp.concatenate([rate, jnp.zeros((1, LANES), F32)], axis=1)
    row = row_iota(CY, NX)

    level_ids = row_iota(LEV, NX)
    for side in range(2):
        if side == 0:
            here = [before_ref[comp, 1] for comp in range(COMP)]
            south = [before_ref[comp, 0] for comp in range(COMP)]
            north = [low_ref[comp, 0] for comp in range(COMP)]
        else:
            here = [after_ref[comp, 0] for comp in range(COMP)]
            south = [high_ref[comp, 1] for comp in range(COMP)]
            north = [after_ref[comp, 1] for comp in range(COMP)]
        for comp in range(COMP):
            u = here[comp]
            below = jnp.where(level_ids == 0, -u, pltpu.roll(u, 1, 0))
            above = jnp.where(level_ids == LEV - 1, u, pltpu.roll(u, LEV - 1, 0))
            west, east = pltpu.roll(u, 1, 1), pltpu.roll(u, NX - 1, 1)
            moved = change(u, here[0], here[1], west, east, north[comp], south[comp], above, below)
            edge_ref[side, comp] = u + moved - rate * u

    for lev in range(LEV):
        stream, cross = fields_ref[0, 0, lev], fields_ref[0, 1, lev]
        loss = rate + drag * jnp.abs(stream) if 1 <= lev <= LEV // 2 else rate
        for comp in range(COMP):
            u = fields_ref[0, comp, lev]
            below = -u if lev == 0 else fields_ref[0, comp, lev - 1]
            above = u if lev == LEV - 1 else fields_ref[0, comp, lev + 1]
            north = jnp.where(row == CY - 1, after_ref[comp, 0, lev : lev + 1, :], pltpu.roll(u, CY - 1, 0))
            south = jnp.where(row == 0, before_ref[comp, 1, lev : lev + 1, :], pltpu.roll(u, 1, 0))
            west, east = pltpu.roll(u, 1, 1), pltpu.roll(u, NX - 1, 1)
            moved = change(u, stream, cross, west, east, north, south, above, below)
            pred_ref[comp, lev] = u + moved - loss * u

    row = row_iota(CY, LANES)
    lane = lane_iota(CY, LANES)
    for lev in range(LEV):
        stream, cross = pred_ref[0, lev, :, LANES:], pred_ref[1, lev, :, LANES:]
        for comp in range(COMP):
            u = pred_ref[comp, lev, :, LANES:]
            left = pred_ref[comp, lev, :, :LANES]
            below = -u if lev == 0 else pred_ref[comp, lev - 1, :, LANES:]
            above = u if lev == LEV - 1 else pred_ref[comp, lev + 1, :, LANES:]
            north = jnp.where(row == CY - 1, edge_ref[1, comp, lev : lev + 1, LANES:], pltpu.roll(u, CY - 1, 0))
            south = jnp.where(row == 0, edge_ref[0, comp, lev : lev + 1, LANES:], pltpu.roll(u, 1, 0))
            east = pltpu.roll(jnp.where(lane == 0, left, u), LANES - 1, 1)
            west = pltpu.roll(jnp.where(lane == LANES - 1, left, u), 1, 1)
            moved = change(u, stream, cross, west, east, north, south, above, below)
            if 1 <= lev <= LEV // 2:
                moved = moved - drag[:, LANES:] * jnp.abs(stream) * u
            right_ref[comp, lev] = 0.5 * (fields_ref[0, comp, lev, :, LANES:] + u + moved)


def finish_kernel(
    const_ref, fields_ref, planar_ref, pred_ref, edge_ref, right_ref, out_ref, unpacked, target, full, edge, result, sems
):
    drag = const_ref[0:CY, :]
    rate = const_ref[CY : CY + 1, :]
    cosine = const_ref[CY + 1 : CY + 2, :]
    sine = const_ref[CY + 2 : CY + 3, :]

    for lev in range(LEV):
        for half in range(2):
            packed = planar_ref[GROUP_ORDER.index(2 * lev + half)]
            for part in range(4):
                turned = packed if part == 0 else pltpu.roll(packed, LANES - part * FR, 1)
                unpacked[2 * lev + half, 8 * part : 8 * part + 8, :] = turned
        aims = []
        for comp in range(COMP):
            parts = []
            for half in range(2):
                origin = comp if comp < 2 else half
                kind = 2 if comp == 2 else (half + comp) % 2
                parts.append(unpacked[2 * lev + origin, pl.ds(kind, HALF, stride=4), :])
            aims.append(jnp.concatenate(parts, axis=0))
        aims = [cosine * aims[0] - sine * aims[1], sine * aims[0] + cosine * aims[1], aims[2]]
        for comp in range(COMP):
            pull = rate * aims[comp]
            target[comp, lev] = pull
            full[comp, lev] = pred_ref[comp, lev, :, :LANES] + pull
    outer = [
        jnp.concatenate([planar_ref[GROUP_ORDER.index(2 * lev + at), 3:4, :] for lev in range(LEV)], axis=0) for at in range(2)
    ]
    for side in range(2):
        aims = []
        for comp in range(COMP):
            origin = comp if comp < 2 else side
            kind = 2 if comp == 2 else (side + comp) % 2
            packed = outer[origin]
            aims.append(packed if kind == 0 else pltpu.roll(packed, LANES - kind * FR, 1))
        aims = [cosine * aims[0] - sine * aims[1], sine * aims[0] + cosine * aims[1], aims[2]]
        for comp in range(COMP):
            edge[side, comp] = edge_ref[side, comp, :, :LANES] + rate * aims[comp]

    row = row_iota(CY, LANES)
    lane = lane_iota(CY, LANES)
    copies = []
    for lev in range(LEV):
        stream, cross = full[0, lev], full[1, lev]
        loss = rate + drag * jnp.abs(stream) if 1 <= lev <= LEV // 2 else rate
        last = 0.05 * (1.0 - pred_ref[0, lev, :, LANES:])
        for comp in range(COMP):
            u = full[comp, lev]
            right = pred_ref[comp, lev, :, LANES:]
            pull = target[comp, lev]
            below = -u if lev == 0 else full[comp, lev - 1]
            above = u if lev == LEV - 1 else full[comp, lev + 1]
            north = jnp.where(row == CY - 1, edge[1, comp, lev : lev + 1, :], pltpu.roll(u, CY - 1, 0))
            south = jnp.where(row == 0, edge[0, comp, lev : lev + 1, :], pltpu.roll(u, 1, 0))
            east = pltpu.roll(jnp.where(lane == 0, right, u), LANES - 1, 1)
            west = pltpu.roll(jnp.where(lane == LANES - 1, right, u), 1, 1)
            moved = change(u, stream, cross, west, east, north, south, above, below) + (pull - loss * u)
            result[comp, lev, :, :LANES] = 0.5 * (fields_ref[0, comp, lev, :, :LANES] + u + moved)
            passed = jnp.where(lane == LANES - 1, pltpu.roll(pull, LANES - 1, 1), 0.0)
            result[comp, lev, :, LANES:] = right_ref[comp, lev] + last * passed
        copy = pltpu.make_async_copy(result.at[:, lev], out_ref.at[0, :, lev], sems.at[lev])
        copy.start()
        copies.append(copy)
    for copy in copies:
        copy.wait()


def local(fields, sample_index, stencil, stencil_weight):
    message, low, high = pl.pallas_call(
        pack_kernel,
        out_shape=(shape(GROUPS, CY, LANES), shape(COMP, 2, LEV, NX), shape(COMP, 2, LEV, NX)),
        in_specs=[HBM, HBM],
        out_specs=(VMEM, VMEM, VMEM),
        scratch_shapes=[
            pltpu.SMEM((1, COMP), jnp.int32),
            pltpu.VMEM((2, COMP, LEV * CY, LANES), F32),
            pltpu.SemaphoreType.DMA((7,)),
        ],
        compiler_params=params(PACK_KIB),
        name="pack",
    )(sample_index, fields.reshape(COMP, LEV * CY, NX))
    up = [(i, (i + 1) % TILES) for i in range(TILES)]
    down = [(j, i) for i, j in up]
    after = lax.ppermute(low, "tile", down)
    before = lax.ppermute(high, "tile", up)
    asked = lax.all_to_all(message, "group", 0, 0, tiled=True)
    hot, spread = pl.pallas_call(
        prepare_kernel,
        out_shape=(
            shape(NY, 2 * CELLS * LANES, dtype=BF16),
            shape(2 * FR, 2 * CELLS * LANES),
        ),
        in_specs=[HBM, HBM],
        out_specs=(VMEM, VMEM),
        scratch_shapes=[
            pltpu.VMEM((2, NYAW, HALF, LANES), jnp.int32),
            pltpu.VMEM((2, NYAW, HALF, LANES), F32),
            pltpu.VMEM((2, NYAW, HALF, LANES), jnp.int32),
            pltpu.VMEM((2, NYAW, HALF, LANES), F32),
            pltpu.VMEM((512, 512), BF16),
            pltpu.SemaphoreType.DMA((2, 4)),
        ],
        compiler_params=params(),
        cost_estimate=cost(100_000_000_000, 200_000),
        name="prepare",
    )(stencil, stencil_weight)
    band = lax.all_to_all(
        jnp.broadcast_to(asked[0:1, :HALF], (TILES, HALF, LANES)),
        "tile",
        0,
        0,
        axis_index_groups=[TILE_ORDER],
        tiled=True,
    )
    pred, edge, right, const = pl.pallas_call(
        begin_kernel,
        out_shape=(
            shape(COMP, LEV, CY, NX),
            shape(2, COMP, LEV, NX),
            shape(COMP, LEV, CY, LANES),
            shape(CY + 8, LANES),
        ),
        in_specs=[SMEM] + [VMEM] * 5,
        out_specs=(VMEM, VMEM, VMEM, VMEM),
        compiler_params=params(),
        cost_estimate=cost(8_000_000, 1_000_000),
        name="begin",
    )(sample_index, fields, high, low, after, before)
    band, pred, edge, right, const = lax.optimization_barrier((band, pred, edge, right, const))
    answers = pl.pallas_call(
        interpolate_kernel,
        out_shape=shape(GROUPS, 8, LANES),
        in_specs=[VMEM] * 4,
        out_specs=VMEM,
        scratch_shapes=[
            pltpu.VMEM((NYAW * 8 * FR, NY), BF16),
            pltpu.VMEM((NYAW * NYAW, 8, LANES), F32),
            pltpu.VMEM((16, LANES), F32),
        ],
        compiler_params=params(),
        name="interpolate",
    )(band, asked, hot, spread)
    planar = lax.all_to_all(answers, "group", 0, 0, axis_index_groups=[GROUP_ORDER], tiled=True)
    return pl.pallas_call(
        finish_kernel,
        out_shape=shape(1, COMP, LEV, CY, NX),
        in_specs=[VMEM] * 6,
        out_specs=HBM,
        scratch_shapes=[
            pltpu.VMEM((2 * LEV, 4 * HALF, LANES), F32),
            pltpu.VMEM((COMP, LEV, CY, LANES), F32),
            pltpu.VMEM((COMP, LEV, CY, LANES), F32),
            pltpu.VMEM((2, COMP, LEV, LANES), F32),
            pltpu.VMEM((COMP, LEV, CY, NX), F32),
            pltpu.SemaphoreType.DMA((LEV,)),
        ],
        compiler_params=params(),
        name="finish",
    )(const, fields, planar, pred, edge, right)


def solution(mesh):
    in_specs = (P("group", None, None, "tile", None), P("group", None), P(), P())
    out_specs = P("group", None, None, "tile", None)
    return jax.shard_map(local, mesh=mesh, in_specs=in_specs, out_specs=out_specs, check_vma=False)
```
